512 devices in a mesh: node: 32 (over x, z_lo, core), state: 16 (over y, z_hi).
Axes of the slice: x: 4, y: 4, z: 16 (z_hi: 4, z_lo: 4; z = z_hi * 4 + z_lo), core: 2. Of those that a mesh axis runs over, the one named last changes fastest.
Arguments:
- states: float32 [24576, 12288], P('node', 'state'), may hold values from -0.0390625 to 0.0390625
- coeffs: float32 [12288, 512], P('state'), may hold values from -6 to 6
- cell_matrix: float32 [384, 125, 125], P('node'), may hold values from -0.5 to 0.5
- connect: int32 [384, 125], P('node'), may hold values from 0 to 831, as said below
- face_list: int32 [2048], P('node'), may hold values from 0 to 767, as said below
- node_mass: float32 [24576], P('node'), may hold values from 0.25 to 4
Outputs:
- rotated: float32 [512, 24576], P('state', 'node')
- h_panel: float32 [512, 12288], P('node', 'state')
- m_panel: float32 [512, 12288], P('node', 'state')
The draws below stay inside these ranges and needn't reach their ends.
Inputs may be any that keep to these rules, and one draw needn't show every extreme that they name: `connect`: within each partition the cells cover a periodic in-plane slab of hexahedral elements of order 4; indices 768 and above name ghosts, every ghost and every owned node is used by some cell. `face_list`: the 64 entries of one partition are distinct.
All inputs are finite; a program needn't handle non-finite values.
Results may differ from the reference program's by a relative error of at most 0.000084.
Values sent between devices are 32-bit elements; how exact they have to be, the bound alone decides.
No kernel may reach another device: no remote copies, remote signals or barrier semaphores. Data moves between devices by JAX's collectives and lax.ppermute only.
A program may use at most 64 MiB of HBM per device.

```python
import math
import jax
import jax.numpy as jnp
from jax import lax

ORDER = 4
NPE = 125
CXY = 2
CZC = 3
NXY = 8
LAYERS = 12
NODES_DEV = 768
FACE = 64
CELLS_DEV = 12
NODES = 24576
STATES = 12288
BLOCK = 512
N_NODE = 32


def node_labels(key):
    keys = jax.vmap(lambda index: jax.random.fold_in(key, index))(jnp.arange(N_NODE))
    return jax.vmap(lambda single: jax.random.permutation(single, NODES_DEV))(keys).astype(jnp.int32)


def grid_axis(position, count):
    extents = (CZC, CXY, CXY, ORDER + 1, ORDER + 1, ORDER + 1)
    shape = [1, 1, 1, 1, 1, 1]
    shape[position] = count
    values = jnp.arange(count, dtype=jnp.int32).reshape(shape)
    return jnp.broadcast_to(values, extents).reshape(-1)


def draw_connect(key, part):
    labels = node_labels(key)
    layer = ORDER * grid_axis(0, CZC) + grid_axis(3, ORDER + 1)
    column = (ORDER * grid_axis(1, CXY) + grid_axis(4, ORDER + 1)) % NXY
    across = (ORDER * grid_axis(2, CXY) + grid_axis(5, ORDER + 1)) % NXY
    planar = column * NXY + across
    canonical = jnp.minimum(layer * NXY * NXY + planar, NODES_DEV - 1).astype(jnp.int32)
    is_ghost = layer == LAYERS
    ghost_index = (NODES_DEV + planar).astype(jnp.int32)
    local = jnp.where(is_ghost[None, :], ghost_index[None, :], labels[:, canonical])
    return local.reshape(N_NODE * CELLS_DEV, NPE).astype(jnp.int32)


def draw_face_list(key, part):
    labels = node_labels(key)
    return labels[:, :FACE].reshape(N_NODE * FACE).astype(jnp.int32)


def steps_of(stream_key, shape, split, smallest, largest):
    def one(dim, blocks):
        draws = jax.random.uniform(jax.random.fold_in(jax.random.fold_in(stream_key, 6), dim), (blocks,), jnp.float32, smallest / len(split), largest / len(split))
        return jnp.repeat(jnp.exp(draws), shape[dim] // blocks).reshape((-1,) + (1,) * (len(shape) - dim - 1))

    level = one(*split[0])
    for cut in split[1:]:
        level = level * one(*cut)
    return level


def bell_draw(key, shape, spread, bound, shards=(), kind=jnp.bfloat16):
    drawn = spread * jax.random.normal(key, shape, jnp.float32)
    if shards:
        drawn = drawn * steps_of(key, shape, shards, -0.22, 0.18)
    return jnp.clip(drawn, -bound, bound).astype(kind)


def setup_inputs(seed: int = 0) -> dict:
    streams_of = jax.random.split(jax.random.key(seed), 7)
    return {
        "states": bell_draw(streams_of[0], (NODES, STATES), NODES ** -0.5, 0.0390625, ((0, 32), (1, 16)), jnp.float32),
        "coeffs": bell_draw(streams_of[1], (STATES, BLOCK), 1.0, 6.0, ((0, 16),), jnp.float32),
        "cell_matrix": bell_draw(streams_of[2], (CELLS_DEV * N_NODE, NPE, NPE), NPE ** -0.5, 0.5, ((0, 32),), jnp.float32),
        "connect": draw_connect(jax.random.fold_in(streams_of[6], 71), 0),
        "face_list": draw_face_list(jax.random.fold_in(streams_of[6], 71), 0),
        "node_mass": jnp.clip(jnp.exp(math.log(4.0) - 2.7725887 * jax.random.uniform(streams_of[5], (NODES,), jnp.float32) ** steps_of(streams_of[5], (NODES,), ((0, 32),), -0.2, 0.2)), 0.25, 4.0),
    }


def apply_cells(block_rows, cell_matrix, connect, face_list):
    height = block_rows.shape[0]
    per_node = block_rows.reshape(height, N_NODE, NODES_DEV)
    face_sets = face_list.reshape(N_NODE, FACE)
    linkage = connect.reshape(N_NODE, CELLS_DEV, NPE)
    element = cell_matrix.reshape(N_NODE, CELLS_DEV, NPE, NPE)
    element = 0.5 * (element + jnp.swapaxes(element, 2, 3))
    face_values = jax.vmap(lambda values, picks: values[:, picks], in_axes=(1, 0), out_axes=1)(per_node, face_sets)
    ghosts = jnp.concatenate([face_values[:, 1:], jnp.zeros((height, 1, FACE), jnp.float32)], axis=1)
    extended = jnp.concatenate([per_node, ghosts], axis=2)

    def per_part(values, links, cells):
        cell_values = values[:, links]
        cell_output = jnp.einsum("cab,rcb->rca", cells, cell_values, precision=lax.Precision.HIGHEST)
        empty = jnp.zeros((height, NODES_DEV + FACE), jnp.float32)
        return empty.at[:, links.reshape(-1)].add(cell_output.reshape(height, -1))

    assembled = jax.vmap(per_part, in_axes=(1, 0, 0), out_axes=1)(extended, linkage, element)
    owned = assembled[:, :, :NODES_DEV]
    returned = jnp.concatenate([jnp.zeros((height, 1, FACE), jnp.float32), assembled[:, :-1, NODES_DEV:]], axis=1)
    owned = jax.vmap(lambda values, picks, extra: values.at[:, picks].add(extra), in_axes=(1, 0, 1), out_axes=1)(owned, face_sets, returned)
    return owned.reshape(height, NODES)


def reference(states, coeffs, cell_matrix, connect, face_list, node_mass):
    rotated = lax.dot_general(coeffs, states, (((0,), (1,)), ((), ())), precision=lax.Precision.HIGHEST, preferred_element_type=jnp.float32)
    applied = apply_cells(rotated, cell_matrix, connect, face_list)
    h_panel = jnp.dot(applied, states, precision=lax.Precision.HIGHEST, preferred_element_type=jnp.float32)
    m_panel = jnp.dot(rotated * node_mass[None, :], states, precision=lax.Precision.HIGHEST, preferred_element_type=jnp.float32)
    return rotated, h_panel, m_panel
```

```python
import jax
import jax.numpy as jnp
from jax import lax
from jax.sharding import Mesh, PartitionSpec as P

FINE = ("x", "zl", "core", "y", "zh")
NODE = ("x", "zl", "core")
STATE = ("y", "zh")
HIGH = lax.Precision.HIGH


def node_shift(shard, by):
    length = lax.axis_size(NODE)
    pairs = [(i, i + by) for i in range(length) if 0 <= i + by < length]
    return lax.ppermute(shard, NODE, pairs)


def ring(shard, axis, by):
    length = lax.axis_size(axis)
    return lax.ppermute(shard, axis, [(i, (i + by) % length) for i in range(length)])


def halves(value):
    top = lax.reduce_precision(value, 8, 7)
    return top.astype(jnp.bfloat16), (value - top).astype(jnp.bfloat16)


def pick(table, value, dims):
    top, low = halves(value)
    dot = lambda part: lax.dot_general(
        table, part, (dims, ((), ())), preferred_element_type=jnp.float32
    )
    return dot(top) + dot(low)


def apply_cells(values, cell_matrix, connect, face_list):
    owned, width = values.shape
    cells, per_cell = connect.shape
    face = face_list.shape[0]
    face_table = (face_list[:, None] == jnp.arange(owned)[None, :]).astype(jnp.bfloat16)
    table = (
        connect.reshape(-1)[:, None] == jnp.arange(owned + face)[None, :]
    ).astype(jnp.bfloat16)
    ghosts = node_shift(pick(face_table, values, ((1,), (0,))), -1)
    extended = jnp.concatenate([values, ghosts], axis=0)
    cell_values = pick(table, extended, ((1,), (0,))).reshape(cells, per_cell, width)
    symmetric = 0.5 * (cell_matrix + jnp.swapaxes(cell_matrix, 1, 2))
    cell_output = jnp.einsum("cab,cbr->car", symmetric, cell_values, precision=HIGH)
    assembled = pick(table, cell_output.reshape(cells * per_cell, width), ((0,), (0,)))
    returned = node_shift(assembled[owned:], 1)
    return assembled[:owned] + pick(face_table, returned, ((0,), (0,)))


def spread_sum(pieces, axis):
    return jnp.sum(lax.all_to_all(pieces, axis, 0, 0, tiled=True), axis=0)


def gather_rows(rows, axis):
    length = lax.axis_size(axis)
    here = lax.axis_index(axis)
    out = jnp.zeros((length,) + rows.shape, rows.dtype)
    out = lax.dynamic_update_slice_in_dim(out, rows[None], here, 0)
    for by in (1, length - 1, 2):
        out = lax.dynamic_update_slice_in_dim(
            out, ring(rows, axis, by)[None], (here - by) % length, 0
        )
    return out


def local(states, coeffs, cell_matrix, connect, face_list, node_mass):
    owned, width = states.shape
    block = coeffs.shape[1]
    partial = lax.dot_general(
        coeffs,
        states,
        (((0,), (1,)), ((), ())),
        precision=HIGH,
        preferred_element_type=jnp.float32,
    )
    over_y = spread_sum(partial.reshape(4, block // 4, owned), "y")
    rotated = spread_sum(over_y.reshape(4, block // 16, owned), "zh")

    weighted = jnp.concatenate(
        [
            apply_cells(states, cell_matrix, connect, face_list),
            states * node_mass[:, None],
        ],
        axis=1,
    )

    group = lax.all_gather(rotated, "zh", axis=0, tiled=False)
    rows = gather_rows(group, "y")
    rows = rows.reshape(16, 2, block // 32, owned).swapaxes(0, 1).reshape(block, owned)
    panel = jnp.dot(rows, weighted, precision=HIGH, preferred_element_type=jnp.float32)
    panel = spread_sum(panel.reshape(2, block // 2, 2 * width), "core")
    panel = spread_sum(panel.reshape(4, block // 8, 2 * width), "x")
    panel = spread_sum(panel.reshape(4, block // 32, 2 * width), "zl")
    return rotated, panel[:, :width], panel[:, width:]


def solution(mesh):
    fine = Mesh(mesh.devices.reshape(4, 4, 2, 4, 4), FINE)
    return jax.shard_map(
        local,
        mesh=fine,
        in_specs=(
            P(NODE, STATE),
            P(STATE, None),
            P(NODE, None, None),
            P(NODE, None),
            P(NODE),
            P(NODE),
        ),
        out_specs=(P(STATE, NODE), P(NODE, STATE), P(NODE, STATE)),
        check_vma=False,
    )
```

```python
import functools

import jax
import jax.numpy as jnp
from jax import lax
from jax.experimental import pallas as pl
from jax.experimental.pallas import tpu as pltpu
from jax.sharding import Mesh, PartitionSpec as P

FINE = ("x", "zl", "core", "y", "zh")
NODE = ("x", "zl", "core")
STATE = ("y", "zh")
VMEM = 40 * 1024 * 1024
F32 = jnp.float32
BF16 = jnp.bfloat16


def node_shift(shard, by):
    length = lax.axis_size(NODE)
    pairs = [(i, i + by) for i in range(length) if 0 <= i + by < length]
    return lax.ppermute(shard, NODE, pairs)


def ring(shard, axis, by):
    length = lax.axis_size(axis)
    return lax.ppermute(shard, axis, [(i, (i + by) % length) for i in range(length)])


def halves(value):
    top = lax.reduce_precision(value, 8, 7)
    return top.astype(BF16), (value - top).astype(BF16)


def split(value):
    top = value.astype(BF16)
    return top, (value - top.astype(F32)).astype(BF16)


def dot(left, right, dims=((1,), (0,))):
    return lax.dot_general(left, right, (dims, ((), ())), preferred_element_type=F32)


def rotate_kernel(coeffs_ref, states_ref, out_ref, top_ref, low_ref):
    @pl.when(pl.program_id(0) == 0)
    def _():
        top, low = split(coeffs_ref[...].T)
        top_ref[...] = top
        low_ref[...] = low

    top, low = split(states_ref[...])
    dims = ((1,), (1,))
    out_ref[...] = (
        dot(top_ref[...], top, dims)
        + dot(low_ref[...], top, dims)
        + dot(top_ref[...], low, dims)
    )


def rotate(coeffs, states):
    width, block = coeffs.shape
    owned = states.shape[0]
    tile = 256
    return pl.pallas_call(
        rotate_kernel,
        grid=(owned // tile,),
        in_specs=[
            pl.BlockSpec((width, block), lambda i: (0, 0)),
            pl.BlockSpec((tile, width), lambda i: (i, 0)),
        ],
        out_specs=pl.BlockSpec((block, tile), lambda i: (0, i)),
        out_shape=jax.ShapeDtypeStruct((block, owned), F32),
        scratch_shapes=[pltpu.VMEM((block, width), BF16)] * 2,
        compiler_params=pltpu.CompilerParams(vmem_limit_bytes=VMEM),
        cost_estimate=pl.CostEstimate(
            flops=6 * block * owned * width, bytes_accessed=6000000, transcendentals=0
        ),
        name="rotate",
    )(coeffs, states)


def cells_kernel(column_ref, row_ref, cell_ref, states_ref, ghost_ref, out_ref, top_ref, low_ref):
    owned = states_ref.shape[0]
    total = out_ref.shape[0]

    @pl.when(pl.program_id(0) == 0)
    def _():
        for lo, hi, ref in ((0, owned, states_ref), (owned, total, ghost_ref)):
            top, low = split(ref[...])
            top_ref[lo:hi] = top
            low_ref[lo:hi] = low
        out_ref[...] = jnp.zeros_like(out_ref)

    two = column_ref.shape[1]
    side = two // 2
    gather = (
        lax.broadcasted_iota(jnp.int32, (two, total), 1) == column_ref[0]
    ).astype(F32).astype(BF16)
    scatter = (
        lax.broadcasted_iota(jnp.int32, (total, two), 0) == row_ref[0]
    ).astype(F32).astype(BF16)
    values = dot(gather, top_ref[...]) + dot(gather, low_ref[...])
    top, low = split(values)
    results = []
    for k in range(2):
        cell = cell_ref[k]
        cell_top, cell_low = split(0.5 * (cell + cell.T))
        rows = slice(k * side, (k + 1) * side)
        results.append(
            dot(cell_top, top[rows]) + dot(cell_low, top[rows]) + dot(cell_top, low[rows])
        )
    top, low = split(jnp.concatenate(results, axis=0))
    out_ref[...] += dot(scatter, top) + dot(scatter, low)


def cells_apply(states, ghosts, cell_matrix, connect):
    owned, width = states.shape
    total = owned + ghosts.shape[0]
    cells, per_cell = connect.shape
    side = 128
    pad = side - per_cell
    cell = jnp.pad(cell_matrix, ((0, 0), (0, pad), (0, pad)))
    links = jnp.pad(connect, ((0, 0), (0, pad)), constant_values=-1)
    steps = cells // 2
    return pl.pallas_call(
        cells_kernel,
        grid=(steps,),
        in_specs=[
            pl.BlockSpec((1, 2 * side, 1), lambda i: (i, 0, 0)),
            pl.BlockSpec((1, 1, 2 * side), lambda i: (i, 0, 0)),
            pl.BlockSpec((2, side, side), lambda i: (i, 0, 0)),
            pl.BlockSpec((owned, width), lambda i: (0, 0)),
            pl.BlockSpec((total - owned, width), lambda i: (0, 0)),
        ],
        out_specs=pl.BlockSpec((total, width), lambda i: (0, 0)),
        out_shape=jax.ShapeDtypeStruct((total, width), F32),
        scratch_shapes=[pltpu.VMEM((total, width), BF16)] * 2,
        compiler_params=pltpu.CompilerParams(vmem_limit_bytes=VMEM),
        cost_estimate=pl.CostEstimate(
            flops=8 * cells * side * total * width, bytes_accessed=9000000, transcendentals=0
        ),
        name="cells",
    )(
        links.reshape(steps, 2 * side, 1),
        links.reshape(steps, 1, 2 * side),
        cell,
        states,
        ghosts,
    )


def face_pick(table, value, dims):
    top, low = halves(value)
    return dot(table, top, dims) + dot(table, low, dims)


def weights(states, cell_matrix, connect, face_list, node_mass):
    owned = states.shape[0]
    table = (face_list[:, None] == jnp.arange(owned)[None, :]).astype(BF16)
    ghosts = node_shift(face_pick(table, states, ((1,), (0,))), -1)
    assembled = cells_apply(states, ghosts, cell_matrix, connect)
    returned = node_shift(assembled[owned:], 1)
    applied = assembled[:owned] + face_pick(table, returned, ((0,), (0,)))
    return jnp.concatenate([applied, states * node_mass[:, None]], axis=1)


def panel_kernel(base_ref, p0, p1, p2, p3, top0, top1, low0, low1, out_ref, top_ref, low_ref):
    rows = p0.shape[0]
    depth = top0.shape[0]

    @pl.when(pl.program_id(0) == 0)
    def _():
        for by, piece in enumerate((p0, p1, p2, p3)):
            place = pl.ds(pl.multiple_of(lax.rem(base_ref[0] + by, 4) * rows, rows), rows)
            top, low = split(piece[...])
            top_ref[place] = top
            low_ref[place] = low

    first, second = slice(0, depth), slice(depth, 2 * depth)
    out_ref[...] = (
        dot(top_ref[:, first], top0[...])
        + dot(low_ref[:, first], top0[...])
        + dot(top_ref[:, first], low0[...])
        + dot(top_ref[:, second], top1[...])
        + dot(low_ref[:, second], top1[...])
        + dot(top_ref[:, second], low1[...])
    )


def panel_dot(base, pieces, tops, lows):
    rows, depth = pieces[0].shape
    width = tops[0].shape[1]
    tile = 256
    whole = pl.BlockSpec((rows, depth), lambda i: (0, 0))
    tall = pl.BlockSpec((depth // 2, tile), lambda i: (0, i))
    return pl.pallas_call(
        panel_kernel,
        grid=(width // tile,),
        in_specs=[pl.BlockSpec(memory_space=pltpu.SMEM)] + [whole] * 4 + [tall] * 4,
        out_specs=pl.BlockSpec((4 * rows, tile), lambda i: (0, i)),
        out_shape=jax.ShapeDtypeStruct((4 * rows, width), F32),
        scratch_shapes=[pltpu.VMEM((4 * rows, depth), BF16)] * 2,
        compiler_params=pltpu.CompilerParams(vmem_limit_bytes=VMEM),
        cost_estimate=pl.CostEstimate(
            flops=6 * 4 * rows * depth * width, bytes_accessed=12000000, transcendentals=0
        ),
        name="panel",
    )(base, *pieces, *tops, *lows)


def spread_sum(pieces, axis):
    return jnp.sum(lax.all_to_all(pieces, axis, 0, 0, tiled=True), axis=0)


def local(states, coeffs, cell_matrix, connect, face_list, node_mass):
    owned, width = states.shape
    block = coeffs.shape[1]
    partial = rotate(coeffs, states)
    over_y = spread_sum(partial.reshape(4, block // 4, owned), "y")
    rotated = spread_sum(over_y.reshape(4, block // 16, owned), "zh")

    late, _ = lax.optimization_barrier((states, partial))
    mine = weights(late, cell_matrix, connect, face_list, node_mass)
    other = ring(mine, "core", 1)
    tops, lows = zip(halves(mine), halves(other))

    core = lax.axis_index("core")
    pair = rotated.reshape(2, block // 32, owned)
    keep = lax.dynamic_index_in_dim(pair, core, 0, keepdims=False)
    send = lax.dynamic_index_in_dim(pair, 1 - core, 0, keepdims=False)
    both = jnp.concatenate([keep, ring(send, "core", 1)], axis=1)
    group = lax.all_gather(both, "zh", axis=0, tiled=False)
    here = lax.axis_index("y")
    results = []
    for half in range(2):
        rows = group[:, half * 8 : (half + 1) * 8].reshape(32, 2 * owned)
        pieces = [rows] + [ring(rows, "y", -by) for by in (1, 2, 3)]
        panel = panel_dot(here.reshape(1).astype(jnp.int32), pieces, tops, lows)
        panel = spread_sum(panel.reshape(4, 32, 2 * width), "x")
        results.append(spread_sum(panel.reshape(4, 8, 2 * width), "zl"))
    panel = jnp.concatenate(results, axis=0)
    return rotated, panel[:, :width], panel[:, width:]


def solution(mesh):
    fine = Mesh(mesh.devices.reshape(4, 4, 2, 4, 4), FINE)
    return jax.shard_map(
        local,
        mesh=fine,
        in_specs=(
            P(NODE, STATE),
            P(STATE, None),
            P(NODE, None, None),
            P(NODE, None),
            P(NODE),
            P(NODE),
        ),
        out_specs=(P(STATE, NODE), P(NODE, STATE), P(NODE, STATE)),
        check_vma=False,
    )
```

```python
import jax
import jax.numpy as jnp
from jax import lax
from jax.experimental import pallas as pl
from jax.experimental.pallas import tpu as pltpu
from jax.sharding import Mesh, PartitionSpec as P

FINE = ("x", "zl", "core", "y", "zh")
NODE = ("x", "zl", "core")
STATE = ("y", "zh")
VMEM = 56 * 1024 * 1024
F32 = jnp.float32
BF16 = jnp.bfloat16


def node_shift(shard, by):
    length = lax.axis_size(NODE)
    pairs = [(i, i + by) for i in range(length) if 0 <= i + by < length]
    return lax.ppermute(shard, NODE, pairs)


def ring(shard, axis, by):
    length = lax.axis_size(axis)
    return lax.ppermute(shard, axis, [(i, (i + by) % length) for i in range(length)])


def halves(value):
    top = lax.reduce_precision(value, 8, 7)
    return top.astype(BF16), (value - top).astype(BF16)


def split(value):
    top = value.astype(BF16)
    return top, (value - top.astype(F32)).astype(BF16)


def dot(left, right, dims=((1,), (0,))):
    return lax.dot_general(left, right, (dims, ((), ())), preferred_element_type=F32)


def params():
    return pltpu.CompilerParams(vmem_limit_bytes=VMEM)


def cost(flops, moved):
    return pl.CostEstimate(flops=flops, bytes_accessed=moved, transcendentals=0)


ANY = pl.BlockSpec(memory_space=pl.ANY)


def rotate_kernel(coeffs_ref, states_ref, out_ref, top_ref, low_ref):
    @pl.when(pl.program_id(0) == 0)
    def _():
        top, low = split(coeffs_ref[...].T)
        for y in range(4):
            for zh in range(4):
                for core in range(2):
                    source = ((y * 4 + zh) * 2 + core) * 16
                    place = ((y * 2 + core) * 4 + zh) * 16
                    top_ref[place : place + 16] = top[source : source + 16]
                    low_ref[place : place + 16] = low[source : source + 16]

    top, low = split(states_ref[...])
    dims = ((1,), (1,))
    out_ref[...] = (
        dot(top_ref[...], top, dims)
        + dot(low_ref[...], top, dims)
        + dot(top_ref[...], low, dims)
    )


def rotate(coeffs, states):
    width, block = coeffs.shape
    owned = states.shape[0]
    tile = 256
    return pl.pallas_call(
        rotate_kernel,
        grid=(owned // tile,),
        in_specs=[
            pl.BlockSpec((width, block), lambda i: (0, 0)),
            pl.BlockSpec((tile, width), lambda i: (i, 0)),
        ],
        out_specs=pl.BlockSpec((block, tile), lambda i: (0, i)),
        out_shape=jax.ShapeDtypeStruct((block, owned), F32),
        scratch_shapes=[pltpu.VMEM((block, width), BF16)] * 2,
        compiler_params=params(),
        cost_estimate=cost(6 * block * owned * width, 6000000),
        name="rotate",
    )(coeffs, states)


def cells_kernel(column_ref, row_ref, cell_ref, states_ref, ghost_ref, _, out_ref, pair_ref):
    owned = states_ref.shape[0]
    total = out_ref.shape[0]
    depth = pair_ref.shape[0] // 2

    @pl.when(pl.program_id(0) == 0)
    def _():
        for place, ref in ((0, states_ref), (owned, ghost_ref)):
            top, low = split(ref[...])
            end = place + ref.shape[0]
            pair_ref[place:end] = top
            pair_ref[depth + place : depth + end] = low
        blank = jnp.zeros((depth - total, pair_ref.shape[1]), BF16)
        pair_ref[total:depth] = blank
        pair_ref[depth + total :] = blank
        out_ref[...] = jnp.zeros_like(out_ref)

    count, side = cell_ref.shape[0], cell_ref.shape[1]
    many = count * side
    gather = (
        lax.broadcasted_iota(jnp.int32, (many, depth), 1) == column_ref[0]
    ).astype(F32).astype(BF16)
    scatter = (
        lax.broadcasted_iota(jnp.int32, (total, many), 0) == row_ref[0]
    ).astype(F32).astype(BF16)
    top, low = split(dot(jnp.concatenate([gather, gather], axis=1), pair_ref[...]))
    results = []
    for k in range(count):
        cell = cell_ref[k]
        cell_top, cell_low = split(0.5 * (cell + cell.T))
        rows = slice(k * side, (k + 1) * side)
        results.append(
            dot(
                jnp.concatenate([cell_top, cell_low, cell_top], axis=1),
                jnp.concatenate([top[rows], top[rows], low[rows]], axis=0),
            )
        )
    top, low = split(jnp.concatenate(results, axis=0))
    out_ref[...] += dot(
        jnp.concatenate([scatter, scatter], axis=1), jnp.concatenate([top, low], axis=0)
    )


def cells_apply(states, ghosts, cell_matrix, connect, after):
    owned, width = states.shape
    total = owned + ghosts.shape[0]
    depth = -(-total // 128) * 128
    cells, per_cell = connect.shape
    side, count = 128, 4
    pad = side - per_cell
    cell = jnp.pad(cell_matrix, ((0, 0), (0, pad), (0, pad)))
    links = jnp.pad(connect, ((0, 0), (0, pad)), constant_values=-1)
    steps = cells // count
    return pl.pallas_call(
        cells_kernel,
        grid=(steps,),
        in_specs=[
            pl.BlockSpec((1, count * side, 1), lambda i: (i, 0, 0)),
            pl.BlockSpec((1, 1, count * side), lambda i: (i, 0, 0)),
            pl.BlockSpec((count, side, side), lambda i: (i, 0, 0)),
            pl.BlockSpec((owned, width), lambda i: (0, 0)),
            pl.BlockSpec((total - owned, width), lambda i: (0, 0)),
            ANY,
        ],
        out_specs=pl.BlockSpec((total, width), lambda i: (0, 0)),
        out_shape=jax.ShapeDtypeStruct((total, width), F32),
        scratch_shapes=[pltpu.VMEM((2 * depth, width), BF16)],
        compiler_params=params(),
        cost_estimate=cost(8 * cells * side * total * width, 9000000),
        name="cells",
    )(
        links.reshape(steps, count * side, 1),
        links.reshape(steps, 1, count * side),
        cell,
        states,
        ghosts,
        after,
    )


def face_pick(table, value, dims):
    top, low = halves(value)
    return dot(table, top, dims) + dot(table, low, dims)


def weights(states, cell_matrix, connect, face_list, node_mass, after):
    owned = states.shape[0]
    table = (face_list[:, None] == jnp.arange(owned)[None, :]).astype(BF16)
    ghosts = node_shift(face_pick(table, states, ((1,), (0,))), -1)
    assembled = cells_apply(states, ghosts, cell_matrix, connect, after)
    returned = node_shift(assembled[owned:], 1)
    applied = assembled[:owned] + face_pick(table, returned, ((0,), (0,)))
    return jnp.concatenate([applied, states * node_mass[:, None]], axis=1)


def panel_kernel(base_ref, p0, p1, p2, p3, mine_ref, other_ref, out_ref, top_ref, low_ref):
    rows = p0.shape[0]
    depth = mine_ref.shape[0]

    @pl.when(pl.program_id(0) == 0)
    def _():
        for by, piece in enumerate((p0, p1, p2, p3)):
            place = pl.ds(pl.multiple_of(lax.rem(base_ref[0] + by, 4) * rows, rows), rows)
            top, low = split(piece[...])
            top_ref[place] = top
            low_ref[place] = low

    total = None
    for k, ref in enumerate((mine_ref, other_ref)):
        top, low = split(ref[...])
        part = slice(k * depth, (k + 1) * depth)
        value = (
            dot(top_ref[:, part], top) + dot(low_ref[:, part], top) + dot(top_ref[:, part], low)
        )
        total = value if total is None else total + value
    out_ref[...] = total


def panel_dot(base, pieces, mine, other):
    rows, depth = pieces[0].shape
    width = mine.shape[1]
    tile = 256
    whole = pl.BlockSpec((rows, depth), lambda i: (0, 0))
    tall = pl.BlockSpec((depth // 2, tile), lambda i: (0, i))
    return pl.pallas_call(
        panel_kernel,
        grid=(width // tile,),
        in_specs=[pl.BlockSpec(memory_space=pltpu.SMEM)] + [whole] * 4 + [tall] * 2,
        out_specs=pl.BlockSpec((4 * rows, tile), lambda i: (0, i)),
        out_shape=jax.ShapeDtypeStruct((4 * rows, width), F32),
        scratch_shapes=[pltpu.VMEM((4 * rows, depth), BF16)] * 2,
        compiler_params=params(),
        cost_estimate=cost(6 * 4 * rows * depth * width, 12000000),
        name="panel",
    )(base, *pieces, mine, other)


def fold_kernel(core_ref, pieces_ref, _, out_ref):
    owned = pieces_ref.shape[3]
    for k in range(2):
        which = core_ref[0] if k == 0 else 1 - core_ref[0]
        value = pieces_ref[0, which]
        for y in range(1, 4):
            value = value + pieces_ref[y, which]
        out_ref[:, k * owned : (k + 1) * owned] = value


def fold(core, pieces, after):
    _, _, rows, owned = pieces.shape
    return pl.pallas_call(
        fold_kernel,
        in_specs=[
            pl.BlockSpec(memory_space=pltpu.SMEM),
            pl.BlockSpec(memory_space=pltpu.VMEM),
            ANY,
        ],
        out_specs=pl.BlockSpec(memory_space=pltpu.VMEM),
        out_shape=jax.ShapeDtypeStruct((rows, 2 * owned), F32),
        compiler_params=params(),
        cost_estimate=cost(8 * rows * owned, 2000000),
        name="fold",
    )(core, pieces, after)


def swap(pieces, axis):
    return lax.all_to_all(pieces, axis, 0, 0, tiled=True)


def local(states, coeffs, cell_matrix, connect, face_list, node_mass):
    owned, width = states.shape
    block = coeffs.shape[1]
    core = lax.axis_index("core").astype(jnp.int32).reshape(1)
    here = lax.axis_index("y").astype(jnp.int32).reshape(1)

    partial = rotate(coeffs, states)
    mine = weights(states, cell_matrix, connect, face_list, node_mass, partial)
    other = ring(mine, "core", 1)
    pieces = swap(partial.reshape(8, block // 8, owned), ("y", "core"))
    over_y = fold(core, pieces.reshape(4, 2, block // 8, owned), mine)
    both = jnp.sum(swap(over_y.reshape(4, block // 32, 2 * owned), "zh"), axis=0)

    own, theirs = both[:, :owned], ring(both[:, owned:], "core", 1)
    first = core[0] == 0
    rotated = jnp.concatenate(
        [jnp.where(first, own, theirs), jnp.where(first, theirs, own)], axis=0
    )

    group = lax.all_gather(both, "zh", axis=0, tiled=True)
    rows = [group] + [ring(group, "y", -by) for by in (1, 2, 3)]
    panel = panel_dot(here, rows, mine, other)
    panel = jnp.sum(swap(panel.reshape(4, block // 8, 2 * width), "x"), axis=0)
    panel = swap(panel.reshape(4, block // 32, 2 * width), "zl")
    return rotated, jnp.sum(panel[:, :, :width], axis=0), jnp.sum(panel[:, :, width:], axis=0)


def solution(mesh):
    fine = Mesh(mesh.devices.reshape(4, 4, 2, 4, 4), FINE)
    return jax.shard_map(
        local,
        mesh=fine,
        in_specs=(
            P(NODE, STATE),
            P(STATE, None),
            P(NODE, None, None),
            P(NODE, None),
            P(NODE),
            P(NODE),
        ),
        out_specs=(P(STATE, NODE), P(NODE, STATE), P(NODE, STATE)),
        check_vma=False,
    )
```

```python
import jax
import jax.numpy as jnp
from jax import lax
from jax.experimental import pallas as pl
from jax.experimental.pallas import tpu as pltpu
from jax.sharding import Mesh, PartitionSpec as P

FINE = ("x", "zl", "core", "y", "zh")
NODE = ("x", "zl", "core")
STATE = ("y", "zh")
VMEM = 56 * 1024 * 1024
F32 = jnp.float32
BF16 = jnp.bfloat16
HIGH = lax.Precision.HIGH


def node_shift(shard, by):
    length = lax.axis_size(NODE)
    pairs = [(i, i + by) for i in range(length) if 0 <= i + by < length]
    return lax.ppermute(shard, NODE, pairs)


def ring(shard, axis, by):
    length = lax.axis_size(axis)
    return lax.ppermute(shard, axis, [(i, (i + by) % length) for i in range(length)])


def halves(value):
    top = lax.reduce_precision(value, 8, 7)
    return top.astype(BF16), (value - top).astype(BF16)


def split(value):
    top = value.astype(BF16)
    return top, (value - top.astype(F32)).astype(BF16)


def dot(left, right, dims=((1,), (0,))):
    return lax.dot_general(left, right, (dims, ((), ())), preferred_element_type=F32)


def params():
    return pltpu.CompilerParams(vmem_limit_bytes=VMEM)


def cost(flops, moved):
    return pl.CostEstimate(flops=flops, bytes_accessed=moved, transcendentals=0)


ANY = pl.BlockSpec(memory_space=pl.ANY)


def rotate_kernel(
    coeffs_ref,
    states_ref,
    connect_ref,
    face_ref,
    mass_ref,
    out_ref,
    links_ref,
    table_ref,
    scale_ref,
    top_ref,
    low_ref,
):
    @pl.when(pl.program_id(0) == 0)
    def _():
        links_ref[...] = connect_ref[...]
        table_ref[...] = face_ref[...]
        scale_ref[...] = mass_ref[...]
        top, low = split(coeffs_ref[...].T)
        for y in range(4):
            for zh in range(4):
                for core in range(2):
                    source = ((y * 4 + zh) * 2 + core) * 16
                    place = ((y * 2 + core) * 4 + zh) * 16
                    top_ref[place : place + 16] = top[source : source + 16]
                    low_ref[place : place + 16] = low[source : source + 16]

    top, low = split(states_ref[...])
    dims = ((1,), (1,))
    out_ref[...] = (
        dot(top_ref[...], top, dims)
        + dot(low_ref[...], top, dims)
        + dot(top_ref[...], low, dims)
    )


def rotate(coeffs, states, connect, face_list, node_mass):
    width, block = coeffs.shape
    owned = states.shape[0]
    tile = 256
    fixed = lambda shape: pl.BlockSpec(shape, lambda i: (0, 0))
    small = [connect, face_list.reshape(1, -1), node_mass.reshape(1, -1)]
    return pl.pallas_call(
        rotate_kernel,
        grid=(owned // tile,),
        in_specs=[
            fixed((width, block)),
            pl.BlockSpec((tile, width), lambda i: (i, 0)),
        ]
        + [fixed(a.shape) for a in small],
        out_specs=[
            pl.BlockSpec((block, tile), lambda i: (0, i)),
        ]
        + [fixed(a.shape) for a in small],
        out_shape=[
            jax.ShapeDtypeStruct((block, owned), F32),
        ]
        + [jax.ShapeDtypeStruct(a.shape, a.dtype) for a in small],
        scratch_shapes=[pltpu.VMEM((block, width), BF16)] * 2,
        compiler_params=params(),
        cost_estimate=cost(6 * block * owned * width, 6000000),
        name="rotate",
    )(coeffs, states, *small)


def cells_kernel(connect_ref, cell_ref, states_ref, ghost_ref, out_ref, pair_ref, link_ref, h_ref):
    owned = states_ref.shape[0]
    total, width = out_ref.shape
    depth = pair_ref.shape[0] // 2
    cells, per_cell = connect_ref.shape
    side, count = h_ref.shape[1], h_ref.shape[0]
    many = count * side

    for place, ref in ((0, states_ref), (owned, ghost_ref)):
        top, low = split(ref[...])
        end = place + ref.shape[0]
        pair_ref[place:end] = top
        pair_ref[depth + place : depth + end] = low
    blank = jnp.zeros((depth - total, width), BF16)
    pair_ref[total:depth] = blank
    pair_ref[depth + total :] = blank
    link_ref[...] = jnp.full(link_ref.shape, -1.0, F32)
    link_ref[:cells, :per_cell] = connect_ref[...].astype(F32)
    h_ref[...] = jnp.zeros_like(h_ref)
    links = link_ref[...]
    columns = links.T
    along = lax.broadcasted_iota(jnp.int32, (side, depth), 1).astype(F32)
    down = lax.broadcasted_iota(jnp.int32, (total, side), 0).astype(F32)

    for first in range(0, cells, count):
        group = range(first, first + count)
        gather = jnp.concatenate(
            [(along == columns[:, c : c + 1]).astype(F32).astype(BF16) for c in group], axis=0
        )
        scatter = jnp.concatenate(
            [(down == links[c : c + 1]).astype(F32).astype(BF16) for c in group], axis=1
        )
        top, low = split(dot(jnp.concatenate([gather, gather], axis=1), pair_ref[...]))
        results = []
        for k, c in enumerate(group):
            h_ref[k, :per_cell, :per_cell] = cell_ref[c]
            cell = h_ref[k]
            cell_top, cell_low = split(0.5 * (cell + cell.T))
            rows = slice(k * side, (k + 1) * side)
            results.append(
                dot(
                    jnp.concatenate([cell_top, cell_low, cell_top], axis=1),
                    jnp.concatenate([top[rows], top[rows], low[rows]], axis=0),
                )
            )
        top, low = split(jnp.concatenate(results, axis=0))
        value = dot(
            jnp.concatenate([scatter, scatter], axis=1), jnp.concatenate([top, low], axis=0)
        )
        out_ref[...] = value if first == 0 else out_ref[...] + value


def cells_apply(states, ghosts, cell_matrix, connect):
    owned, width = states.shape
    total = owned + ghosts.shape[0]
    depth = -(-total // 128) * 128
    cells = connect.shape[0]
    side, count = 128, 4
    return pl.pallas_call(
        cells_kernel,
        out_shape=jax.ShapeDtypeStruct((total, width), F32),
        in_specs=[pl.BlockSpec(memory_space=pltpu.VMEM)] * 4,
        out_specs=pl.BlockSpec(memory_space=pltpu.VMEM),
        scratch_shapes=[
            pltpu.VMEM((2 * depth, width), BF16),
            pltpu.VMEM((16, side), F32),
            pltpu.VMEM((count, side, side), F32),
        ],
        compiler_params=params(),
        cost_estimate=cost(8 * cells * side * total * width, 9000000),
        name="cells",
    )(connect, cell_matrix, states, ghosts)


def face_pick(table, value, dims):
    top, low = halves(value)
    return dot(table, top, dims) + dot(table, low, dims)


def tie_kernel(*refs):
    pass


def tie(*arrays):
    return pl.pallas_call(
        tie_kernel,
        in_specs=[ANY] * len(arrays),
        out_specs=[ANY] * len(arrays),
        out_shape=[jax.ShapeDtypeStruct(a.shape, a.dtype) for a in arrays],
        input_output_aliases={i: i for i in range(len(arrays))},
        name="tie",
    )(*arrays)


def swap(pieces, axis):
    return lax.all_to_all(pieces, axis, 0, 0, tiled=True)


def spread_sum(pieces, axis):
    length = lax.axis_size(axis)
    here = lax.axis_index(axis)
    part = lambda by: lax.dynamic_index_in_dim(pieces, (here + by) % length, 0, keepdims=False)
    return sum((ring(part(by), axis, by) for by in range(1, length)), part(0))


def gather_rows(rows, axis):
    length = lax.axis_size(axis)
    here = lax.axis_index(axis)
    out = jnp.zeros((length,) + rows.shape, rows.dtype)
    out = lax.dynamic_update_slice_in_dim(out, rows[None], here, 0)
    for by in (1, length - 1, 2):
        out = lax.dynamic_update_slice_in_dim(
            out, ring(rows, axis, by)[None], (here - by) % length, 0
        )
    return out.reshape((-1,) + rows.shape[1:])


def local(states, coeffs, cell_matrix, connect, face_list, node_mass):
    owned, width = states.shape
    block = coeffs.shape[1]
    first = lax.axis_index("core") == 0

    partial, links, faces, mass = rotate(coeffs, states, connect, face_list, node_mass)
    pieces = swap(partial.reshape(8, block // 8, owned), ("y", "core"))

    weighted = states * mass.reshape(-1, 1)
    weighted_other = ring(weighted, "core", 1)
    table = (faces.reshape(-1, 1) == jnp.arange(owned)[None, :]).astype(BF16)
    ghosts = node_shift(face_pick(table, states, ((1,), (0,))), -1)
    assembled = cells_apply(states, ghosts, cell_matrix, links)

    over_y = jnp.sum(pieces.reshape(4, 2, block // 8, owned), axis=0)
    over_y = jnp.concatenate(
        [jnp.where(first, over_y[0], over_y[1]), jnp.where(first, over_y[1], over_y[0])], axis=1
    )
    over_y, assembled = tie(over_y, assembled)
    both = jnp.sum(swap(over_y.reshape(4, block // 32, 2 * owned), "zh"), axis=0)

    returned = node_shift(assembled[owned:], 1)
    applied = assembled[:owned] + face_pick(table, returned, ((0,), (0,)))
    parts = 4
    applied_other = jnp.concatenate(
        [ring(part, "core", 1) for part in jnp.split(applied, parts, axis=0)], axis=0
    )

    own, theirs = both[:, :owned], ring(both[:, owned:], "core", 1)
    rotated = jnp.concatenate(
        [jnp.where(first, own, theirs), jnp.where(first, theirs, own)], axis=0
    )

    rows = gather_rows(lax.all_gather(both, "zh", axis=0, tiled=True), "y")

    def panel(here, there):
        return sum(
            jnp.dot(part, weight, precision=HIGH, preferred_element_type=F32)
            for part, weight in ((rows[:, :owned], here), (rows[:, owned:], there))
        ).reshape(4, block // 8, width)

    def over_x(value):
        return jnp.sum(swap(value, "x"), axis=0).reshape(4, block // 32, width)

    m_panel = spread_sum(over_x(panel(weighted, weighted_other)), "zl")
    h_panel = jnp.sum(swap(over_x(panel(applied, applied_other)), "zl"), axis=0)
    return rotated, h_panel, m_panel


def solution(mesh):
    fine = Mesh(mesh.devices.reshape(4, 4, 2, 4, 4), FINE)
    return jax.shard_map(
        local,
        mesh=fine,
        in_specs=(
            P(NODE, STATE),
            P(STATE, None),
            P(NODE, None, None),
            P(NODE, None),
            P(NODE),
            P(NODE),
        ),
        out_specs=(P(STATE, NODE), P(NODE, STATE), P(NODE, STATE)),
        check_vma=False,
    )
```

```python
import functools

import jax
import jax.numpy as jnp
from jax import lax
from jax.experimental import pallas as pl
from jax.experimental.pallas import tpu as pltpu
from jax.sharding import Mesh, PartitionSpec as P

FINE = ("x", "zl", "core", "y", "zh")
NODE = ("x", "zl", "core")
STATE = ("y", "zh")
VMEM = 56 * 1024 * 1024
F32 = jnp.float32
BF16 = jnp.bfloat16
HIGH = lax.Precision.HIGH


def node_shift(shard, by):
    length = lax.axis_size(NODE)
    pairs = [(i, i + by) for i in range(length) if 0 <= i + by < length]
    return lax.ppermute(shard, NODE, pairs)


def ring(shard, axis, by):
    length = lax.axis_size(axis)
    return lax.ppermute(shard, axis, [(i, (i + by) % length) for i in range(length)])


def halves(value):
    top = lax.reduce_precision(value, 8, 7)
    return top.astype(BF16), (value - top).astype(BF16)


def split(value):
    top = value.astype(BF16)
    return top, (value - top.astype(F32)).astype(BF16)


def dot(left, right, dims=((1,), (0,))):
    return lax.dot_general(left, right, (dims, ((), ())), preferred_element_type=F32)


def params():
    return pltpu.CompilerParams(vmem_limit_bytes=VMEM)


def cost(flops, moved):
    return pl.CostEstimate(flops=flops, bytes_accessed=moved, transcendentals=0)


ANY = pl.BlockSpec(memory_space=pl.ANY)


def rotate_kernel(
    coeffs_ref, states_ref, face_ref, out_ref, picked_ref, top_ref, low_ref
):
    step = pl.program_id(0)
    tile = states_ref.shape[0]

    @pl.when(step == 0)
    def _():
        top, low = split(coeffs_ref[...].T)
        top_ref[...] = top
        low_ref[...] = low
        picked_ref[...] = jnp.zeros_like(picked_ref)

    top, low = split(states_ref[...])
    dims = ((1,), (1,))
    out_ref[...] = (
        dot(top_ref[...], top, dims)
        + dot(low_ref[...], top, dims)
        + dot(top_ref[...], low, dims)
    )
    nodes = lax.broadcasted_iota(jnp.int32, (face_ref.shape[0], tile), 1) + step * tile
    table = (nodes == face_ref[...]).astype(F32).astype(BF16)
    picked_ref[...] += dot(table, top) + dot(table, low)


def rotate(coeffs, states, face_list):
    width, block = coeffs.shape
    owned = states.shape[0]
    face = face_list.shape[0]
    tile = 256
    fixed = lambda shape: pl.BlockSpec(shape, lambda i: (0, 0))
    return pl.pallas_call(
        rotate_kernel,
        grid=(owned // tile,),
        in_specs=[
            fixed((width, block)),
            pl.BlockSpec((tile, width), lambda i: (i, 0)),
            fixed((face, 1)),
        ],
        out_specs=[
            pl.BlockSpec((block, tile), lambda i: (0, i)),
            fixed((face, width)),
        ],
        out_shape=[
            jax.ShapeDtypeStruct((block, owned), F32),
            jax.ShapeDtypeStruct((face, width), F32),
        ],
        scratch_shapes=[pltpu.VMEM((block, width), BF16)] * 2,
        compiler_params=params(),
        cost_estimate=cost(6 * block * owned * width, 6000000),
        name="rotate",
    )(coeffs, states, face_list.reshape(-1, 1))


def cells_kernel(some, connect_ref, cell_ref, states_ref, ghost_ref, *refs):
    before_ref = refs[0] if len(refs) == 5 else None
    out_ref, pair_ref, link_ref, h_ref = refs[-4:]
    owned = states_ref.shape[0]
    total, width = out_ref.shape
    depth = pair_ref.shape[0] // 2
    cells, per_cell = connect_ref.shape
    side, count = h_ref.shape[1], h_ref.shape[0]
    many = count * side

    for place, ref in ((0, states_ref), (owned, ghost_ref)):
        top, low = split(ref[...])
        end = place + ref.shape[0]
        pair_ref[place:end] = top
        pair_ref[depth + place : depth + end] = low
    blank = jnp.zeros((depth - total, width), BF16)
    pair_ref[total:depth] = blank
    pair_ref[depth + total :] = blank
    link_ref[...] = jnp.full(link_ref.shape, -1.0, F32)
    link_ref[:cells, :per_cell] = connect_ref[...].astype(F32)
    h_ref[...] = jnp.zeros_like(h_ref)
    links = link_ref[...]
    columns = links.T
    along = lax.broadcasted_iota(jnp.int32, (side, depth), 1).astype(F32)
    down = lax.broadcasted_iota(jnp.int32, (total, side), 0).astype(F32)

    for first in range(some.start, some.stop, count):
        group = range(first, first + count)
        gather = jnp.concatenate(
            [(along == columns[:, c : c + 1]).astype(F32).astype(BF16) for c in group], axis=0
        )
        scatter = jnp.concatenate(
            [(down == links[c : c + 1]).astype(F32).astype(BF16) for c in group], axis=1
        )
        top, low = split(dot(jnp.concatenate([gather, gather], axis=1), pair_ref[...]))
        results = []
        for k, c in enumerate(group):
            h_ref[k, :per_cell, :per_cell] = cell_ref[c]
            cell = h_ref[k]
            cell_top, cell_low = split(0.5 * (cell + cell.T))
            rows = slice(k * side, (k + 1) * side)
            results.append(
                dot(
                    jnp.concatenate([cell_top, cell_low, cell_top], axis=1),
                    jnp.concatenate([top[rows], top[rows], low[rows]], axis=0),
                )
            )
        top, low = split(jnp.concatenate(results, axis=0))
        value = dot(
            jnp.concatenate([scatter, scatter], axis=1), jnp.concatenate([top, low], axis=0)
        )
        if first > some.start:
            out_ref[...] += value
        elif before_ref is not None:
            out_ref[...] = before_ref[...] + value
        else:
            out_ref[...] = value


def cells_apply(some, states, ghosts, cell_matrix, connect, *before):
    owned, width = states.shape
    total = owned + ghosts.shape[0]
    depth = -(-total // 128) * 128
    side, count = 128, 3
    arrays = (connect, cell_matrix, states, ghosts) + before
    return pl.pallas_call(
        functools.partial(cells_kernel, some),
        out_shape=jax.ShapeDtypeStruct((total, width), F32),
        in_specs=[pl.BlockSpec(memory_space=pltpu.VMEM)] * len(arrays),
        out_specs=pl.BlockSpec(memory_space=pltpu.VMEM),
        scratch_shapes=[
            pltpu.VMEM((2 * depth, width), BF16),
            pltpu.VMEM((16, side), F32),
            pltpu.VMEM((count, side, side), F32),
        ],
        compiler_params=params(),
        cost_estimate=cost(8 * len(some) * side * total * width, 9000000),
        name="cells",
    )(*arrays)


def face_pick(table, value, dims):
    top, low = halves(value)
    return dot(table, top, dims) + dot(table, low, dims)


def tie_kernel(*refs):
    pass


def tie(*arrays):
    return pl.pallas_call(
        tie_kernel,
        in_specs=[ANY] * len(arrays),
        out_specs=[ANY] * len(arrays),
        out_shape=[jax.ShapeDtypeStruct(a.shape, a.dtype) for a in arrays],
        input_output_aliases={i: i for i in range(len(arrays))},
        name="tie",
    )(*arrays)


def swap(pieces, axis):
    return lax.all_to_all(pieces, axis, 0, 0, tiled=True)


def gather_rows(rows, axis):
    length = lax.axis_size(axis)
    here = lax.axis_index(axis)
    out = jnp.zeros((2, length) + rows.shape[1:], rows.dtype)
    out = lax.dynamic_update_slice_in_dim(out, rows[:, None], here, 1)
    for by in (1, length - 1, 2):
        out = lax.dynamic_update_slice_in_dim(
            out, ring(rows, axis, by)[:, None], (here - by) % length, 1
        )
    return out


def local(states, coeffs, cell_matrix, connect, face_list, node_mass):
    owned, width = states.shape
    block = coeffs.shape[1]
    cells = connect.shape[0]
    first = lax.axis_index("core") == 0

    partial, picked = rotate(coeffs, states, face_list)
    pieces = swap(partial.reshape(4, block // 4, owned), "y")

    ghosts = node_shift(picked, -1)
    some, rest = range(cells // 2), range(cells // 2, cells)
    assembled = cells_apply(some, states, ghosts, cell_matrix, connect)

    over_y, assembled = tie(jnp.sum(pieces, axis=0), assembled)
    rotated = jnp.sum(swap(over_y.reshape(4, block // 16, owned), "zh"), axis=0)

    assembled = cells_apply(rest, states, ghosts, cell_matrix, connect, assembled)
    returned = node_shift(assembled[owned:], 1)
    table = (face_list[:, None] == jnp.arange(owned)[None, :]).astype(BF16)
    applied = assembled[:owned] + face_pick(table, returned, ((0,), (0,)))
    weights = jnp.concatenate([applied, states * node_mass[:, None]], axis=1)

    pair = rotated.reshape(2, block // 32, owned)
    pair = jnp.concatenate(
        [jnp.where(first, pair[1], pair[0]), jnp.where(first, pair[0], pair[1])], axis=0
    )
    group = lax.all_gather(pair, "zh", axis=0, tiled=True)
    group = group.reshape(4, 2, block // 32, owned).swapaxes(0, 1)
    rows = gather_rows(group.reshape(2, block // 8, owned), "y")
    rows = rows.reshape(2, block // 2, owned)
    theirs, ours = (
        jnp.dot(rows[k], weights, precision=HIGH, preferred_element_type=F32) for k in range(2)
    )
    panel = ours + ring(theirs, "core", 1)
    panel = jnp.sum(swap(panel.reshape(4, block // 8, 2 * width), "x"), axis=0)
    panel = swap(panel.reshape(4, block // 32, 2 * width), "zl")
    return rotated, jnp.sum(panel[:, :, :width], axis=0), jnp.sum(panel[:, :, width:], axis=0)


def solution(mesh):
    fine = Mesh(mesh.devices.reshape(4, 4, 2, 4, 4), FINE)
    return jax.shard_map(
        local,
        mesh=fine,
        in_specs=(
            P(NODE, STATE),
            P(STATE, None),
            P(NODE, None, None),
            P(NODE, None),
            P(NODE),
            P(NODE),
        ),
        out_specs=(P(STATE, NODE), P(NODE, STATE), P(NODE, STATE)),
        check_vma=False,
    )
```

```python
import jax
import jax.numpy as jnp
from jax import lax
from jax.experimental import pallas as pl
from jax.experimental.pallas import tpu as pltpu
from jax.sharding import Mesh, PartitionSpec as P

FINE = ("x", "zl", "core", "y", "zh")
NODE = ("x", "zl", "core")
STATE = ("y", "zh")
VMEM = 56 * 1024 * 1024
F32 = jnp.float32
BF16 = jnp.bfloat16
HIGH = lax.Precision.HIGH


def node_shift(shard, by):
    length = lax.axis_size(NODE)
    pairs = [(i, i + by) for i in range(length) if 0 <= i + by < length]
    return lax.ppermute(shard, NODE, pairs)


def ring(shard, axis, by):
    length = lax.axis_size(axis)
    return lax.ppermute(shard, axis, [(i, (i + by) % length) for i in range(length)])


def split(value):
    top = value.astype(BF16)
    return top, (value - top.astype(F32)).astype(BF16)


def dot(left, right, dims=((1,), (0,))):
    return lax.dot_general(left, right, (dims, ((), ())), preferred_element_type=F32)


def params():
    return pltpu.CompilerParams(vmem_limit_bytes=VMEM)


def cost(flops, moved):
    return pl.CostEstimate(flops=flops, bytes_accessed=moved, transcendentals=0)


ANY = pl.BlockSpec(memory_space=pl.ANY)


def face_table(face_ref, start, rows):
    nodes = lax.broadcasted_iota(jnp.int32, (rows, face_ref.shape[1]), 0) + start
    return (nodes == face_ref[...]).astype(F32).astype(BF16)


def rotate_kernel(coeffs_ref, states_ref, face_ref, out_ref, picked_ref, top_ref, low_ref):
    step = pl.program_id(0)
    tile = states_ref.shape[0]

    @pl.when(step == 0)
    def _():
        top, low = split(coeffs_ref[...].T)
        for y in range(4):
            for zh in range(4):
                for core in range(2):
                    source = ((y * 4 + zh) * 2 + core) * 16
                    place = ((y * 2 + core) * 4 + zh) * 16
                    top_ref[place : place + 16] = top[source : source + 16]
                    low_ref[place : place + 16] = low[source : source + 16]
        picked_ref[...] = jnp.zeros_like(picked_ref)

    top, low = split(states_ref[...])
    dims = ((1,), (1,))
    out_ref[...] = (
        dot(top_ref[...], top, dims)
        + dot(low_ref[...], top, dims)
        + dot(top_ref[...], low, dims)
    )
    table = face_table(face_ref, step * tile, tile)
    dims = ((0,), (0,))
    picked_ref[...] += dot(table, top, dims) + dot(table, low, dims)


def rotate(coeffs, states, faces):
    width, block = coeffs.shape
    owned = states.shape[0]
    face = faces.shape[1]
    tile = 256
    fixed = lambda shape: pl.BlockSpec(shape, lambda i: (0, 0))
    return pl.pallas_call(
        rotate_kernel,
        grid=(owned // tile,),
        in_specs=[
            fixed((width, block)),
            pl.BlockSpec((tile, width), lambda i: (i, 0)),
            fixed((1, face)),
        ],
        out_specs=[
            pl.BlockSpec((block, tile), lambda i: (0, i)),
            fixed((face, width)),
        ],
        out_shape=[
            jax.ShapeDtypeStruct((block, owned), F32),
            jax.ShapeDtypeStruct((face, width), F32),
        ],
        scratch_shapes=[pltpu.VMEM((block, width), BF16)] * 2,
        compiler_params=params(),
        cost_estimate=cost(6 * block * owned * width, 6000000),
        name="rotate",
    )(coeffs, states, faces)


def assemble_kernel(connect_ref, cell_ref, _, top_ref, low_ref, sum_ref, link_ref, h_ref):
    total, depth = top_ref.shape
    cells, per_cell = connect_ref.shape
    count, side = h_ref.shape[0], h_ref.shape[1]

    link_ref[...] = jnp.full(link_ref.shape, -1.0, F32)
    link_ref[:cells, :per_cell] = connect_ref[...].astype(F32)
    h_ref[...] = jnp.zeros_like(h_ref)
    links = link_ref[...]
    columns = links.T
    along = lax.broadcasted_iota(jnp.int32, (side, depth), 1).astype(F32)
    down = lax.broadcasted_iota(jnp.int32, (total, side), 0).astype(F32)

    for first in range(0, cells, count):
        scatter, tops, lows = [], [], []
        for k in range(count):
            c = first + k
            gather = (along == columns[:, c : c + 1]).astype(F32).astype(BF16)
            scatter.append((down == links[c : c + 1]).astype(F32).astype(BF16))
            h_ref[k, :per_cell, :per_cell] = cell_ref[c]
            cell = h_ref[k]
            top, low = split(0.5 * (cell + cell.T))
            top, low = split(dot(top, gather) + dot(low, gather))
            tops.append(top)
            lows.append(low)
        value = dot(
            jnp.concatenate(scatter + scatter, axis=1), jnp.concatenate(tops + lows, axis=0)
        )
        if first + count < cells:
            sum_ref[...] = value if first == 0 else sum_ref[...] + value
        else:
            top_ref[...], low_ref[...] = split(sum_ref[...] + value)


def assemble(connect, cell_matrix, total, after):
    depth = -(-total // 128) * 128
    cells = connect.shape[0]
    side, count = 128, 4
    whole = pl.BlockSpec(memory_space=pltpu.VMEM)
    return pl.pallas_call(
        assemble_kernel,
        out_shape=[jax.ShapeDtypeStruct((total, depth), BF16)] * 2,
        in_specs=[whole, whole, ANY],
        out_specs=[whole] * 2,
        scratch_shapes=[
            pltpu.VMEM((total, depth), F32),
            pltpu.VMEM((16, side), F32),
            pltpu.VMEM((count, side, side), F32),
        ],
        compiler_params=params(),
        cost_estimate=cost(8000000000, 4000000),
        name="assemble",
    )(connect, cell_matrix, after)


def extend(states_ref, ghost_ref, depth):
    states, ghosts = states_ref[...], ghost_ref[...]
    rest = depth - states.shape[0] - ghosts.shape[0]
    blank = jnp.zeros((rest, states.shape[1]), BF16)
    pair = split(states), split(ghosts)
    return [jnp.concatenate([pair[0][k], pair[1][k], blank], axis=0) for k in range(2)]


def product(top_ref, low_ref, top, low):
    return dot(top_ref[...], top) + dot(low_ref[...], top) + dot(top_ref[...], low)


def back_kernel(top_ref, low_ref, states_ref, ghost_ref, out_ref):
    out_ref[...] = product(top_ref, low_ref, *extend(states_ref, ghost_ref, top_ref.shape[1]))


def apply_back(matrix, states, ghosts):
    owned, width = states.shape
    face, depth = ghosts.shape[0], matrix[0].shape[1]
    fixed = lambda shape: pl.BlockSpec(shape, lambda i: (0, 0))
    rows = pl.BlockSpec((face, depth), lambda i: (owned // face, 0))
    return pl.pallas_call(
        back_kernel,
        grid=(1,),
        in_specs=[rows, rows, fixed(states.shape), fixed(ghosts.shape)],
        out_specs=fixed(ghosts.shape),
        out_shape=jax.ShapeDtypeStruct(ghosts.shape, F32),
        compiler_params=params(),
        cost_estimate=cost(600000000, 4000000),
        name="back",
    )(*matrix, states, ghosts)


def apply_kernel(
    top_ref, low_ref, states_ref, ghost_ref, mass_ref, back_ref, face_ref, out_ref, scaled_ref
):
    owned = states_ref.shape[0]
    value = product(top_ref, low_ref, *extend(states_ref, ghost_ref, top_ref.shape[1]))
    table = face_table(face_ref, 0, owned)
    top, low = split(back_ref[...])
    out_ref[...] = value + dot(table, top) + dot(table, low)
    side = mass_ref.shape[1]
    for k in range(owned // side):
        column = jnp.broadcast_to(mass_ref[k : k + 1, :], (8, side)).T[:, :1]
        rows = slice(k * side, (k + 1) * side)
        scaled_ref[rows] = states_ref[rows] * column


def apply_cells(matrix, states, ghosts, returned, faces, mass):
    owned, width = states.shape
    depth = matrix[0].shape[1]
    tile, side = 256, 128
    fixed = lambda shape: pl.BlockSpec(shape, lambda i: (0, 0))
    tall = pl.BlockSpec((owned, tile), lambda i: (0, i))
    low = pl.BlockSpec((ghosts.shape[0], tile), lambda i: (0, i))
    return pl.pallas_call(
        apply_kernel,
        grid=(width // tile,),
        in_specs=[fixed((owned, depth))] * 2
        + [tall, low, fixed((owned // side, side)), low, fixed(faces.shape)],
        out_specs=[tall] * 2,
        out_shape=[jax.ShapeDtypeStruct((owned, width), F32)] * 2,
        compiler_params=params(),
        cost_estimate=cost(7000000000, 11000000),
        name="apply",
    )(*matrix, states, ghosts, mass.reshape(-1, side), returned, faces)


def tie_kernel(*refs):
    pass


def tie(*arrays):
    return pl.pallas_call(
        tie_kernel,
        in_specs=[ANY] * len(arrays),
        out_specs=[ANY] * len(arrays),
        out_shape=[jax.ShapeDtypeStruct(a.shape, a.dtype) for a in arrays],
        input_output_aliases={i: i for i in range(len(arrays))},
        name="tie",
    )(*arrays)


def swap(pieces, axis):
    return lax.all_to_all(pieces, axis, 0, 0, tiled=True)


def gather_rows(rows, axis):
    length = lax.axis_size(axis)
    here = lax.axis_index(axis)
    out = jnp.zeros((length,) + rows.shape, rows.dtype)
    out = lax.dynamic_update_slice_in_dim(out, rows[None], here, 0)
    for by in (1, length - 1, 2):
        out = lax.dynamic_update_slice_in_dim(
            out, ring(rows, axis, by)[None], (here - by) % length, 0
        )
    return out.reshape((-1,) + rows.shape[1:])


def local(states, coeffs, cell_matrix, connect, face_list, node_mass):
    owned, width = states.shape
    block = coeffs.shape[1]
    first = lax.axis_index("core") == 0
    faces = face_list.reshape(1, -1)

    partial, picked = rotate(coeffs, states, faces)
    pieces = swap(partial.reshape(8, block // 8, owned), ("y", "core"))
    ghosts = node_shift(picked, -1)
    matrix = assemble(connect, cell_matrix, owned + faces.shape[1], partial)
    returned = node_shift(apply_back(matrix, states, ghosts), 1)

    over_y = jnp.sum(pieces.reshape(4, 2, block // 8, owned), axis=0)
    over_y = jnp.concatenate(
        [jnp.where(first, over_y[0], over_y[1]), jnp.where(first, over_y[1], over_y[0])], axis=1
    )
    over_y, returned, *matrix = tie(over_y, returned, *matrix)
    both = jnp.sum(swap(over_y.reshape(4, block // 32, 2 * owned), "zh"), axis=0)

    mine = apply_cells(matrix, states, ghosts, returned, faces, node_mass)
    other = [ring(weight, "core", 1) for weight in mine]

    own, theirs = both[:, :owned], ring(both[:, owned:], "core", 1)
    rotated = jnp.concatenate(
        [jnp.where(first, own, theirs), jnp.where(first, theirs, own)], axis=0
    )

    rows = gather_rows(lax.all_gather(both, "zh", axis=0, tiled=True), "y")
    panel = jnp.concatenate(
        [
            sum(
                jnp.dot(part, weight, precision=HIGH, preferred_element_type=F32)
                for part, weight in ((rows[:, :owned], here), (rows[:, owned:], there))
            )
            for here, there in zip(mine, other)
        ],
        axis=1,
    )
    panel = jnp.sum(swap(panel.reshape(4, block // 8, 2 * width), "x"), axis=0)
    panel = swap(panel.reshape(4, block // 32, 2 * width), "zl")
    return rotated, jnp.sum(panel[:, :, :width], axis=0), jnp.sum(panel[:, :, width:], axis=0)


def solution(mesh):
    fine = Mesh(mesh.devices.reshape(4, 4, 2, 4, 4), FINE)
    return jax.shard_map(
        local,
        mesh=fine,
        in_specs=(
            P(NODE, STATE),
            P(STATE, None),
            P(NODE, None, None),
            P(NODE, None),
            P(NODE),
            P(NODE),
        ),
        out_specs=(P(STATE, NODE), P(NODE, STATE), P(NODE, STATE)),
        check_vma=False,
    )
```

```python
import jax
import jax.numpy as jnp
from jax import lax
from jax.experimental import pallas as pl
from jax.experimental.pallas import tpu as pltpu
from jax.sharding import Mesh, PartitionSpec as P

FINE = ("x", "zl", "core", "y", "zh")
NODE = ("x", "zl", "core")
STATE = ("y", "zh")
VMEM = 56 * 1024 * 1024
F32 = jnp.float32
BF16 = jnp.bfloat16
HIGH = lax.Precision.HIGH


def node_shift(shard, by):
    length = lax.axis_size(NODE)
    pairs = [(i, i + by) for i in range(length) if 0 <= i + by < length]
    return lax.ppermute(shard, NODE, pairs)


def ring(shard, axis, by):
    length = lax.axis_size(axis)
    return lax.ppermute(shard, axis, [(i, (i + by) % length) for i in range(length)])


def split(value):
    top = value.astype(BF16)
    return top, (value - top.astype(F32)).astype(BF16)


def dot(left, right, dims=((1,), (0,))):
    return lax.dot_general(left, right, (dims, ((), ())), preferred_element_type=F32)


def params():
    return pltpu.CompilerParams(vmem_limit_bytes=VMEM)


def cost(flops, moved):
    return pl.CostEstimate(flops=flops, bytes_accessed=moved, transcendentals=0)


ANY = pl.BlockSpec(memory_space=pl.ANY)


def face_table(face_ref, start, rows):
    nodes = lax.broadcasted_iota(jnp.int32, (rows, face_ref.shape[1]), 0) + start
    return (nodes == face_ref[...]).astype(F32).astype(BF16)


def rotate_kernel(coeffs_ref, states_ref, face_ref, out_ref, picked_ref, top_ref, low_ref):
    step = pl.program_id(0)
    tile = states_ref.shape[0]

    @pl.when(step == 0)
    def _():
        top, low = split(coeffs_ref[...].T)
        for y in range(4):
            for zh in range(4):
                for core in range(2):
                    source = ((y * 4 + zh) * 2 + core) * 16
                    place = ((y * 2 + core) * 4 + zh) * 16
                    top_ref[place : place + 16] = top[source : source + 16]
                    low_ref[place : place + 16] = low[source : source + 16]
        picked_ref[...] = jnp.zeros_like(picked_ref)

    top, low = split(states_ref[...])
    dims = ((1,), (1,))
    out_ref[...] = (
        dot(top_ref[...], top, dims)
        + dot(low_ref[...], top, dims)
        + dot(top_ref[...], low, dims)
    )
    table = face_table(face_ref, step * tile, tile)
    dims = ((0,), (0,))
    picked_ref[...] += dot(table, top, dims) + dot(table, low, dims)


def rotate(coeffs, states, faces):
    width, block = coeffs.shape
    owned = states.shape[0]
    face = faces.shape[1]
    tile = 256
    fixed = lambda shape: pl.BlockSpec(shape, lambda i: (0, 0))
    return pl.pallas_call(
        rotate_kernel,
        grid=(owned // tile,),
        in_specs=[
            fixed((width, block)),
            pl.BlockSpec((tile, width), lambda i: (i, 0)),
            fixed((1, face)),
        ],
        out_specs=[
            pl.BlockSpec((block, tile), lambda i: (0, i)),
            fixed((face, width)),
        ],
        out_shape=[
            jax.ShapeDtypeStruct((block, owned), F32),
            jax.ShapeDtypeStruct((face, width), F32),
        ],
        scratch_shapes=[pltpu.VMEM((block, width), BF16)] * 2,
        compiler_params=params(),
        cost_estimate=cost(6 * block * owned * width, 6000000),
        name="rotate",
    )(coeffs, states, faces)


def assemble_kernel(connect_ref, cell_ref, _, top_ref, low_ref, sum_ref, link_ref, h_ref):
    total, depth = top_ref.shape
    cells, per_cell = connect_ref.shape
    count, side = h_ref.shape[0], h_ref.shape[1]

    link_ref[...] = jnp.full(link_ref.shape, -1.0, F32)
    link_ref[:cells, :per_cell] = connect_ref[...].astype(F32)
    h_ref[...] = jnp.zeros_like(h_ref)
    links = link_ref[...]
    columns = links.T
    along = lax.broadcasted_iota(jnp.int32, (side, depth), 1).astype(F32)
    down = lax.broadcasted_iota(jnp.int32, (total, side), 0).astype(F32)

    for first in range(0, cells, count):
        scatter, tops, lows = [], [], []
        for k in range(count):
            c = first + k
            gather = (along == columns[:, c : c + 1]).astype(F32).astype(BF16)
            scatter.append((down == links[c : c + 1]).astype(F32).astype(BF16))
            h_ref[k, :per_cell, :per_cell] = cell_ref[c]
            cell = h_ref[k]
            top, low = split(0.5 * (cell + cell.T))
            top, low = split(dot(top, gather) + dot(low, gather))
            tops.append(top)
            lows.append(low)
        value = dot(
            jnp.concatenate(scatter + scatter, axis=1), jnp.concatenate(tops + lows, axis=0)
        )
        if first + count < cells:
            sum_ref[...] = value if first == 0 else sum_ref[...] + value
        else:
            top_ref[...], low_ref[...] = split(sum_ref[...] + value)


def assemble(connect, cell_matrix, total, after):
    depth = -(-total // 128) * 128
    cells = connect.shape[0]
    side, count = 128, 4
    whole = pl.BlockSpec(memory_space=pltpu.VMEM)
    return pl.pallas_call(
        assemble_kernel,
        out_shape=[jax.ShapeDtypeStruct((total, depth), BF16)] * 2,
        in_specs=[whole, whole, ANY],
        out_specs=[whole] * 2,
        scratch_shapes=[
            pltpu.VMEM((total, depth), F32),
            pltpu.VMEM((16, side), F32),
            pltpu.VMEM((count, side, side), F32),
        ],
        compiler_params=params(),
        cost_estimate=cost(8000000000, 4000000),
        name="assemble",
    )(connect, cell_matrix, after)


def extend(states_ref, ghost_ref, depth):
    states, ghosts = states_ref[...], ghost_ref[...]
    rest = depth - states.shape[0] - ghosts.shape[0]
    blank = jnp.zeros((rest, states.shape[1]), BF16)
    pair = split(states), split(ghosts)
    return [jnp.concatenate([pair[0][k], pair[1][k], blank], axis=0) for k in range(2)]


def product(top_ref, low_ref, top, low):
    return dot(top_ref[...], top) + dot(low_ref[...], top) + dot(top_ref[...], low)


def back_kernel(top_ref, low_ref, states_ref, ghost_ref, out_ref):
    out_ref[...] = product(top_ref, low_ref, *extend(states_ref, ghost_ref, top_ref.shape[1]))


def apply_back(matrix, states, ghosts):
    owned, width = states.shape
    face, depth = ghosts.shape[0], matrix[0].shape[1]
    fixed = lambda shape: pl.BlockSpec(shape, lambda i: (0, 0))
    rows = pl.BlockSpec((face, depth), lambda i: (owned // face, 0))
    return pl.pallas_call(
        back_kernel,
        grid=(1,),
        in_specs=[rows, rows, fixed(states.shape), fixed(ghosts.shape)],
        out_specs=fixed(ghosts.shape),
        out_shape=jax.ShapeDtypeStruct(ghosts.shape, F32),
        compiler_params=params(),
        cost_estimate=cost(600000000, 4000000),
        name="back",
    )(*matrix, states, ghosts)


def apply_kernel(
    top_ref, low_ref, states_ref, ghost_ref, mass_ref, back_ref, face_ref, out_ref, scaled_ref
):
    owned = states_ref.shape[0]
    value = product(top_ref, low_ref, *extend(states_ref, ghost_ref, top_ref.shape[1]))
    table = face_table(face_ref, 0, owned)
    top, low = split(back_ref[...])
    out_ref[...] = value + dot(table, top) + dot(table, low)
    side = mass_ref.shape[1]
    for k in range(owned // side):
        column = jnp.broadcast_to(mass_ref[k : k + 1, :], (8, side)).T[:, :1]
        rows = slice(k * side, (k + 1) * side)
        scaled_ref[rows] = states_ref[rows] * column


def apply_cells(matrix, states, ghosts, returned, faces, mass):
    owned, width = states.shape
    depth = matrix[0].shape[1]
    tile, side = 256, 128
    fixed = lambda shape: pl.BlockSpec(shape, lambda i: (0, 0))
    tall = pl.BlockSpec((owned, tile), lambda i: (0, i))
    low = pl.BlockSpec((ghosts.shape[0], tile), lambda i: (0, i))
    return pl.pallas_call(
        apply_kernel,
        grid=(width // tile,),
        in_specs=[fixed((owned, depth))] * 2
        + [tall, low, fixed((owned // side, side)), low, fixed(faces.shape)],
        out_specs=[tall] * 2,
        out_shape=[jax.ShapeDtypeStruct((owned, width), F32)] * 2,
        compiler_params=params(),
        cost_estimate=cost(7000000000, 11000000),
        name="apply",
    )(*matrix, states, ghosts, mass.reshape(-1, side), returned, faces)


def tie_kernel(*refs):
    pass


def tie(*arrays):
    return pl.pallas_call(
        tie_kernel,
        in_specs=[ANY] * len(arrays),
        out_specs=[ANY] * len(arrays),
        out_shape=[jax.ShapeDtypeStruct(a.shape, a.dtype) for a in arrays],
        input_output_aliases={i: i for i in range(len(arrays))},
        name="tie",
    )(*arrays)


def swap(pieces, axis):
    return lax.all_to_all(pieces, axis, 0, 0, tiled=True)


def local(states, coeffs, cell_matrix, connect, face_list, node_mass):
    owned, width = states.shape
    block = coeffs.shape[1]
    first = lax.axis_index("core") == 0
    faces = face_list.reshape(1, -1)

    partial, picked = rotate(coeffs, states, faces)
    pieces = swap(partial.reshape(8, block // 8, owned), ("y", "core"))
    ghosts = node_shift(picked, -1)
    matrix = assemble(connect, cell_matrix, owned + faces.shape[1], partial)
    returned = node_shift(apply_back(matrix, states, ghosts), 1)

    over_y = jnp.sum(pieces.reshape(4, 2, block // 8, owned), axis=0)
    over_y = jnp.concatenate(
        [jnp.where(first, over_y[0], over_y[1]), jnp.where(first, over_y[1], over_y[0])], axis=1
    )
    over_y, returned, *matrix = tie(over_y, returned, *matrix)
    both = jnp.sum(swap(over_y.reshape(4, block // 32, 2 * owned), "zh"), axis=0)

    mine = apply_cells(matrix, states, ghosts, returned, faces, node_mass)
    other = [ring(weight, "core", 1) for weight in mine]

    own, theirs = both[:, :owned], ring(both[:, owned:], "core", 1)
    rotated = jnp.concatenate(
        [jnp.where(first, own, theirs), jnp.where(first, theirs, own)], axis=0
    )

    group = lax.all_gather(both, "zh", axis=0, tiled=True)
    rows = swap(jnp.broadcast_to(group[None], (4,) + group.shape), "y")
    rows = rows.reshape(block // 2, 2 * owned)
    panel = jnp.concatenate(
        [
            sum(
                jnp.dot(part, weight, precision=HIGH, preferred_element_type=F32)
                for part, weight in ((rows[:, :owned], here), (rows[:, owned:], there))
            )
            for here, there in zip(mine, other)
        ],
        axis=1,
    )
    panel = jnp.sum(swap(panel.reshape(4, block // 8, 2 * width), "x"), axis=0)
    panel = swap(panel.reshape(4, block // 32, 2 * width), "zl")
    return rotated, jnp.sum(panel[:, :, :width], axis=0), jnp.sum(panel[:, :, width:], axis=0)


def solution(mesh):
    fine = Mesh(mesh.devices.reshape(4, 4, 2, 4, 4), FINE)
    return jax.shard_map(
        local,
        mesh=fine,
        in_specs=(
            P(NODE, STATE),
            P(STATE, None),
            P(NODE, None, None),
            P(NODE, None),
            P(NODE),
            P(NODE),
        ),
        out_specs=(P(STATE, NODE), P(NODE, STATE), P(NODE, STATE)),
        check_vma=False,
    )
```

```python
import jax
import jax.numpy as jnp
from jax import lax
from jax.experimental import pallas as pl
from jax.experimental.pallas import tpu as pltpu
from jax.sharding import Mesh, PartitionSpec as P

FINE = ("x", "zl", "core", "y", "zh")
NODE = ("x", "zl", "core")
STATE = ("y", "zh")
VMEM = 56 * 1024 * 1024
F32 = jnp.float32
BF16 = jnp.bfloat16
HIGH = lax.Precision.HIGH


def node_shift(shard, by):
    length = lax.axis_size(NODE)
    pairs = [(i, i + by) for i in range(length) if 0 <= i + by < length]
    return lax.ppermute(shard, NODE, pairs)


def ring(shard, axis, by):
    length = lax.axis_size(axis)
    return lax.ppermute(shard, axis, [(i, (i + by) % length) for i in range(length)])


def split(value):
    top = value.astype(BF16)
    return top, (value - top.astype(F32)).astype(BF16)


def dot(left, right, dims=((1,), (0,))):
    return lax.dot_general(left, right, (dims, ((), ())), preferred_element_type=F32)


def params():
    return pltpu.CompilerParams(vmem_limit_bytes=VMEM)


def cost(flops, moved):
    return pl.CostEstimate(flops=flops, bytes_accessed=moved, transcendentals=0)


ANY = pl.BlockSpec(memory_space=pl.ANY)


def face_table(face_ref, start, rows):
    nodes = lax.broadcasted_iota(jnp.int32, (rows, face_ref.shape[1]), 0) + start
    return (nodes == face_ref[...]).astype(F32).astype(BF16)


def rotate_kernel(coeffs_ref, states_ref, face_ref, out_ref, picked_ref, top_ref, low_ref):
    step = pl.program_id(0)
    tile = states_ref.shape[0]

    @pl.when(step == 0)
    def _():
        top, low = split(coeffs_ref[...].T)
        for y in range(4):
            for zh in range(4):
                for core in range(2):
                    source = ((y * 4 + zh) * 2 + core) * 16
                    place = ((y * 2 + core) * 4 + zh) * 16
                    top_ref[place : place + 16] = top[source : source + 16]
                    low_ref[place : place + 16] = low[source : source + 16]
        picked_ref[...] = jnp.zeros_like(picked_ref)

    top, low = split(states_ref[...])
    dims = ((1,), (1,))
    out_ref[...] = (
        dot(top_ref[...], top, dims)
        + dot(low_ref[...], top, dims)
        + dot(top_ref[...], low, dims)
    )
    table = face_table(face_ref, step * tile, tile)
    dims = ((0,), (0,))
    picked_ref[...] += dot(table, top, dims) + dot(table, low, dims)


def rotate(coeffs, states, faces):
    width, block = coeffs.shape
    owned = states.shape[0]
    face = faces.shape[1]
    tile = 256
    fixed = lambda shape: pl.BlockSpec(shape, lambda i: (0, 0))
    return pl.pallas_call(
        rotate_kernel,
        grid=(owned // tile,),
        in_specs=[
            fixed((width, block)),
            pl.BlockSpec((tile, width), lambda i: (i, 0)),
            fixed((1, face)),
        ],
        out_specs=[
            pl.BlockSpec((block, tile), lambda i: (0, i)),
            fixed((face, width)),
        ],
        out_shape=[
            jax.ShapeDtypeStruct((block, owned), F32),
            jax.ShapeDtypeStruct((face, width), F32),
        ],
        scratch_shapes=[pltpu.VMEM((block, width), BF16)] * 2,
        compiler_params=params(),
        cost_estimate=cost(6 * block * owned * width, 6000000),
        name="rotate",
    )(coeffs, states, faces)


def assemble_kernel(connect_ref, cell_ref, _, top_ref, low_ref, sum_ref, link_ref, h_ref):
    total, depth = top_ref.shape
    cells, per_cell = connect_ref.shape
    count, side = h_ref.shape[0], h_ref.shape[1]

    link_ref[...] = jnp.full(link_ref.shape, -1.0, F32)
    link_ref[:cells, :per_cell] = connect_ref[...].astype(F32)
    h_ref[...] = jnp.zeros_like(h_ref)
    links = link_ref[...]
    columns = links.T
    along = lax.broadcasted_iota(jnp.int32, (side, depth), 1).astype(F32)
    down = lax.broadcasted_iota(jnp.int32, (total, side), 0).astype(F32)

    for first in range(0, cells, count):
        scatter, tops, lows = [], [], []
        for k in range(count):
            c = first + k
            gather = (along == columns[:, c : c + 1]).astype(F32).astype(BF16)
            scatter.append((down == links[c : c + 1]).astype(F32).astype(BF16))
            h_ref[k, :per_cell, :per_cell] = cell_ref[c]
            cell = h_ref[k]
            top, low = split(0.5 * (cell + cell.T))
            top, low = split(dot(top, gather) + dot(low, gather))
            tops.append(top)
            lows.append(low)
        value = dot(
            jnp.concatenate(scatter + scatter, axis=1), jnp.concatenate(tops + lows, axis=0)
        )
        if first + count < cells:
            sum_ref[...] = value if first == 0 else sum_ref[...] + value
        else:
            top_ref[...], low_ref[...] = split(sum_ref[...] + value)


def assemble(connect, cell_matrix, total, after):
    depth = -(-total // 128) * 128
    cells = connect.shape[0]
    side, count = 128, 4
    whole = pl.BlockSpec(memory_space=pltpu.VMEM)
    return pl.pallas_call(
        assemble_kernel,
        out_shape=[jax.ShapeDtypeStruct((total, depth), BF16)] * 2,
        in_specs=[whole, whole, ANY],
        out_specs=[whole] * 2,
        scratch_shapes=[
            pltpu.VMEM((total, depth), F32),
            pltpu.VMEM((16, side), F32),
            pltpu.VMEM((count, side, side), F32),
        ],
        compiler_params=params(),
        cost_estimate=cost(8000000000, 4000000),
        name="assemble",
    )(connect, cell_matrix, after)


def extend(states_ref, ghost_ref, depth):
    states, ghosts = states_ref[...], ghost_ref[...]
    rest = depth - states.shape[0] - ghosts.shape[0]
    blank = jnp.zeros((rest, states.shape[1]), BF16)
    pair = split(states), split(ghosts)
    return [jnp.concatenate([pair[0][k], pair[1][k], blank], axis=0) for k in range(2)]


def product(top_ref, low_ref, top, low):
    return dot(top_ref[...], top) + dot(low_ref[...], top) + dot(top_ref[...], low)


def back_kernel(top_ref, low_ref, states_ref, ghost_ref, out_ref):
    out_ref[...] = product(top_ref, low_ref, *extend(states_ref, ghost_ref, top_ref.shape[1]))


def apply_back(matrix, states, ghosts):
    owned, width = states.shape
    face, depth = ghosts.shape[0], matrix[0].shape[1]
    tile = 384
    rows = pl.BlockSpec((face, depth), lambda i: (owned // face, 0))
    tall = pl.BlockSpec((owned, tile), lambda i: (0, i))
    low = pl.BlockSpec((face, tile), lambda i: (0, i))
    return pl.pallas_call(
        back_kernel,
        grid=(width // tile,),
        in_specs=[rows, rows, tall, low],
        out_specs=low,
        out_shape=jax.ShapeDtypeStruct(ghosts.shape, F32),
        compiler_params=params(),
        cost_estimate=cost(600000000, 4000000),
        name="back",
    )(*matrix, states, ghosts)


def apply_kernel(
    top_ref, low_ref, states_ref, ghost_ref, mass_ref, back_ref, face_ref, out_ref, scaled_ref
):
    owned = states_ref.shape[0]
    value = product(top_ref, low_ref, *extend(states_ref, ghost_ref, top_ref.shape[1]))
    table = face_table(face_ref, 0, owned)
    top, low = split(back_ref[...])
    out_ref[...] = value + dot(table, top) + dot(table, low)
    side = mass_ref.shape[1]
    for k in range(owned // side):
        column = jnp.broadcast_to(mass_ref[k : k + 1, :], (8, side)).T[:, :1]
        rows = slice(k * side, (k + 1) * side)
        scaled_ref[rows] = states_ref[rows] * column


def apply_cells(matrix, states, ghosts, returned, faces, mass):
    owned, width = states.shape
    depth = matrix[0].shape[1]
    tile, side = 256, 128
    fixed = lambda shape: pl.BlockSpec(shape, lambda i: (0, 0))
    tall = pl.BlockSpec((owned, tile), lambda i: (0, i))
    low = pl.BlockSpec((ghosts.shape[0], tile), lambda i: (0, i))
    return pl.pallas_call(
        apply_kernel,
        grid=(width // tile,),
        in_specs=[fixed((owned, depth))] * 2
        + [tall, low, fixed((owned // side, side)), low, fixed(faces.shape)],
        out_specs=[tall] * 2,
        out_shape=[jax.ShapeDtypeStruct((owned, width), F32)] * 2,
        compiler_params=params(),
        cost_estimate=cost(7000000000, 11000000),
        name="apply",
    )(*matrix, states, ghosts, mass.reshape(-1, side), returned, faces)


def tie_kernel(*refs):
    pass


def tie(*arrays):
    return pl.pallas_call(
        tie_kernel,
        in_specs=[ANY] * len(arrays),
        out_specs=[ANY] * len(arrays),
        out_shape=[jax.ShapeDtypeStruct(a.shape, a.dtype) for a in arrays],
        input_output_aliases={i: i for i in range(len(arrays))},
        name="tie",
    )(*arrays)


def swap(pieces, axis):
    return lax.all_to_all(pieces, axis, 0, 0, tiled=True)


def local(states, coeffs, cell_matrix, connect, face_list, node_mass):
    owned, width = states.shape
    block = coeffs.shape[1]
    first = lax.axis_index("core") == 0
    faces = face_list.reshape(1, -1)

    partial, picked = rotate(coeffs, states, faces)
    pieces = swap(partial.reshape(8, block // 8, owned), ("y", "core"))
    ghosts = node_shift(picked, -1)
    matrix = assemble(connect, cell_matrix, owned + faces.shape[1], partial)
    returned = node_shift(apply_back(matrix, states, ghosts), 1)

    over_y = jnp.sum(pieces.reshape(4, 2, block // 8, owned), axis=0)
    over_y = jnp.concatenate(
        [jnp.where(first, over_y[0], over_y[1]), jnp.where(first, over_y[1], over_y[0])], axis=1
    )
    over_y, returned, *matrix = tie(over_y, returned, *matrix)
    both = jnp.sum(swap(over_y.reshape(4, block // 32, 2 * owned), "zh"), axis=0)

    mine = apply_cells(matrix, states, ghosts, returned, faces, node_mass)
    other = [ring(weight, "core", 1) for weight in mine]

    own, theirs = both[:, :owned], ring(both[:, owned:], "core", 1)
    rotated = jnp.concatenate(
        [jnp.where(first, own, theirs), jnp.where(first, theirs, own)], axis=0
    )

    group = lax.all_gather(both, "zh", axis=0, tiled=True)
    rows = swap(jnp.broadcast_to(group[None], (4,) + group.shape), "y")
    rows = rows.reshape(block // 2, 2 * owned)
    panel = jnp.concatenate(
        [
            sum(
                jnp.dot(part, weight, precision=HIGH, preferred_element_type=F32)
                for part, weight in ((rows[:, :owned], here), (rows[:, owned:], there))
            )
            for here, there in zip(mine, other)
        ],
        axis=1,
    )
    panel = jnp.sum(swap(panel.reshape(4, block // 8, 2 * width), "x"), axis=0)
    panel = swap(panel.reshape(4, block // 32, 2 * width), "zl")
    return rotated, jnp.sum(panel[:, :, :width], axis=0), jnp.sum(panel[:, :, width:], axis=0)


def solution(mesh):
    fine = Mesh(mesh.devices.reshape(4, 4, 2, 4, 4), FINE)
    return jax.shard_map(
        local,
        mesh=fine,
        in_specs=(
            P(NODE, STATE),
            P(STATE, None),
            P(NODE, None, None),
            P(NODE, None),
            P(NODE),
            P(NODE),
        ),
        out_specs=(P(STATE, NODE), P(NODE, STATE), P(NODE, STATE)),
        check_vma=False,
    )
```

```python
import jax
import jax.numpy as jnp
from jax import lax
from jax.experimental import pallas as pl
from jax.experimental.pallas import tpu as pltpu
from jax.sharding import Mesh, PartitionSpec as P

FINE = ("x", "zl", "core", "y", "zh")
NODE = ("x", "zl", "core")
STATE = ("y", "zh")
VMEM = 56 * 1024 * 1024
F32 = jnp.float32
BF16 = jnp.bfloat16
HIGH = lax.Precision.HIGH


def node_shift(shard, by):
    length = lax.axis_size(NODE)
    pairs = [(i, i + by) for i in range(length) if 0 <= i + by < length]
    return lax.ppermute(shard, NODE, pairs)


def ring(shard, axis, by):
    length = lax.axis_size(axis)
    return lax.ppermute(shard, axis, [(i, (i + by) % length) for i in range(length)])


def split(value):
    top = value.astype(BF16)
    return top, (value - top.astype(F32)).astype(BF16)


def dot(left, right, dims=((1,), (0,))):
    return lax.dot_general(left, right, (dims, ((), ())), preferred_element_type=F32)


def params():
    return pltpu.CompilerParams(vmem_limit_bytes=VMEM)


def cost(flops, moved):
    return pl.CostEstimate(flops=flops, bytes_accessed=moved, transcendentals=0)


ANY = pl.BlockSpec(memory_space=pl.ANY)


def face_table(face_ref, start, rows):
    nodes = lax.broadcasted_iota(jnp.int32, (rows, face_ref.shape[1]), 0) + start
    return (nodes == face_ref[...]).astype(F32).astype(BF16)


def rotate_kernel(coeffs_ref, states_ref, face_ref, out_ref, picked_ref, top_ref, low_ref):
    step = pl.program_id(0)
    tile = states_ref.shape[0]

    @pl.when(step == 0)
    def _():
        top, low = split(coeffs_ref[...].T)
        for y in range(4):
            for zh in range(4):
                for core in range(2):
                    source = ((y * 4 + zh) * 2 + core) * 16
                    place = ((y * 2 + core) * 4 + zh) * 16
                    top_ref[place : place + 16] = top[source : source + 16]
                    low_ref[place : place + 16] = low[source : source + 16]
        picked_ref[...] = jnp.zeros_like(picked_ref)

    top, low = split(states_ref[...])
    dims = ((1,), (1,))
    out_ref[...] = (
        dot(top_ref[...], top, dims)
        + dot(low_ref[...], top, dims)
        + dot(top_ref[...], low, dims)
    )
    table = face_table(face_ref, step * tile, tile)
    dims = ((0,), (0,))
    picked_ref[...] += dot(table, top, dims) + dot(table, low, dims)


def rotate(coeffs, states, faces):
    width, block = coeffs.shape
    owned = states.shape[0]
    face = faces.shape[1]
    tile = 768
    fixed = lambda shape: pl.BlockSpec(shape, lambda i: (0, 0))
    return pl.pallas_call(
        rotate_kernel,
        grid=(owned // tile,),
        in_specs=[
            fixed((width, block)),
            pl.BlockSpec((tile, width), lambda i: (i, 0)),
            fixed((1, face)),
        ],
        out_specs=[
            pl.BlockSpec((block, tile), lambda i: (0, i)),
            fixed((face, width)),
        ],
        out_shape=[
            jax.ShapeDtypeStruct((block, owned), F32),
            jax.ShapeDtypeStruct((face, width), F32),
        ],
        scratch_shapes=[pltpu.VMEM((block, width), BF16)] * 2,
        compiler_params=params(),
        cost_estimate=cost(6 * block * owned * width, 6000000),
        name="rotate",
    )(coeffs, states, faces)


def assemble_kernel(connect_ref, cell_ref, _, top_ref, low_ref, sum_ref, link_ref, h_ref):
    total, depth = top_ref.shape
    cells, per_cell = connect_ref.shape
    count, side = h_ref.shape[0], h_ref.shape[1]

    link_ref[...] = jnp.full(link_ref.shape, -1.0, F32)
    link_ref[:cells, :per_cell] = connect_ref[...].astype(F32)
    h_ref[...] = jnp.zeros_like(h_ref)
    links = link_ref[...]
    columns = links.T
    along = lax.broadcasted_iota(jnp.int32, (side, depth), 1).astype(F32)
    down = lax.broadcasted_iota(jnp.int32, (total, side), 0).astype(F32)

    for first in range(0, cells, count):
        scatter, tops, lows = [], [], []
        for k in range(count):
            c = first + k
            gather = (along == columns[:, c : c + 1]).astype(F32).astype(BF16)
            scatter.append((down == links[c : c + 1]).astype(F32).astype(BF16))
            h_ref[k, :per_cell, :per_cell] = cell_ref[c]
            cell = h_ref[k]
            top, low = split(0.5 * (cell + cell.T))
            top, low = split(dot(top, gather) + dot(low, gather))
            tops.append(top)
            lows.append(low)
        value = dot(
            jnp.concatenate(scatter + scatter, axis=1), jnp.concatenate(tops + lows, axis=0)
        )
        if first + count < cells:
            sum_ref[...] = value if first == 0 else sum_ref[...] + value
        else:
            top_ref[...], low_ref[...] = split(sum_ref[...] + value)


def assemble(connect, cell_matrix, total, after):
    depth = -(-total // 128) * 128
    cells = connect.shape[0]
    side, count = 128, 4
    whole = pl.BlockSpec(memory_space=pltpu.VMEM)
    return pl.pallas_call(
        assemble_kernel,
        out_shape=[jax.ShapeDtypeStruct((total, depth), BF16)] * 2,
        in_specs=[whole, whole, ANY],
        out_specs=[whole] * 2,
        scratch_shapes=[
            pltpu.VMEM((total, depth), F32),
            pltpu.VMEM((16, side), F32),
            pltpu.VMEM((count, side, side), F32),
        ],
        compiler_params=params(),
        cost_estimate=cost(8000000000, 4000000),
        name="assemble",
    )(connect, cell_matrix, after)


def extend(states_ref, ghost_ref, depth):
    states, ghosts = states_ref[...], ghost_ref[...]
    rest = depth - states.shape[0] - ghosts.shape[0]
    blank = jnp.zeros((rest, states.shape[1]), BF16)
    pair = split(states), split(ghosts)
    return [jnp.concatenate([pair[0][k], pair[1][k], blank], axis=0) for k in range(2)]


def product(top_ref, low_ref, top, low):
    return dot(top_ref[...], top) + dot(low_ref[...], top) + dot(top_ref[...], low)


def back_kernel(top_ref, low_ref, states_ref, ghost_ref, out_ref):
    out_ref[...] = product(top_ref, low_ref, *extend(states_ref, ghost_ref, top_ref.shape[1]))


def apply_back(matrix, states, ghosts):
    owned, width = states.shape
    face, depth = ghosts.shape[0], matrix[0].shape[1]
    tile = 384
    rows = pl.BlockSpec((face, depth), lambda i: (owned // face, 0))
    tall = pl.BlockSpec((owned, tile), lambda i: (0, i))
    low = pl.BlockSpec((face, tile), lambda i: (0, i))
    return pl.pallas_call(
        back_kernel,
        grid=(width // tile,),
        in_specs=[rows, rows, tall, low],
        out_specs=low,
        out_shape=jax.ShapeDtypeStruct(ghosts.shape, F32),
        compiler_params=params(),
        cost_estimate=cost(600000000, 4000000),
        name="back",
    )(*matrix, states, ghosts)


def apply_kernel(
    top_ref, low_ref, states_ref, ghost_ref, mass_ref, back_ref, face_ref, out_ref, scaled_ref
):
    owned = states_ref.shape[0]
    value = product(top_ref, low_ref, *extend(states_ref, ghost_ref, top_ref.shape[1]))
    table = face_table(face_ref, 0, owned)
    top, low = split(back_ref[...])
    out_ref[...] = value + dot(table, top) + dot(table, low)
    side = mass_ref.shape[1]
    for k in range(owned // side):
        column = jnp.broadcast_to(mass_ref[k : k + 1, :], (8, side)).T[:, :1]
        rows = slice(k * side, (k + 1) * side)
        scaled_ref[rows] = states_ref[rows] * column


def apply_cells(matrix, states, ghosts, returned, faces, mass):
    owned, width = states.shape
    depth = matrix[0].shape[1]
    tile, side = 256, 128
    fixed = lambda shape: pl.BlockSpec(shape, lambda i: (0, 0))
    tall = pl.BlockSpec((owned, tile), lambda i: (0, i))
    low = pl.BlockSpec((ghosts.shape[0], tile), lambda i: (0, i))
    return pl.pallas_call(
        apply_kernel,
        grid=(width // tile,),
        in_specs=[fixed((owned, depth))] * 2
        + [tall, low, fixed((owned // side, side)), low, fixed(faces.shape)],
        out_specs=[tall] * 2,
        out_shape=[jax.ShapeDtypeStruct((owned, width), F32)] * 2,
        compiler_params=params(),
        cost_estimate=cost(7000000000, 11000000),
        name="apply",
    )(*matrix, states, ghosts, mass.reshape(-1, side), returned, faces)


def tie_kernel(*refs):
    pass


def tie(*arrays):
    return pl.pallas_call(
        tie_kernel,
        in_specs=[ANY] * len(arrays),
        out_specs=[ANY] * len(arrays),
        out_shape=[jax.ShapeDtypeStruct(a.shape, a.dtype) for a in arrays],
        input_output_aliases={i: i for i in range(len(arrays))},
        name="tie",
    )(*arrays)


def swap(pieces, axis):
    return lax.all_to_all(pieces, axis, 0, 0, tiled=True)


def local(states, coeffs, cell_matrix, connect, face_list, node_mass):
    owned, width = states.shape
    block = coeffs.shape[1]
    first = lax.axis_index("core") == 0
    faces = face_list.reshape(1, -1)

    partial, picked = rotate(coeffs, states, faces)
    pieces = swap(partial.reshape(8, block // 8, owned), ("y", "core"))
    ghosts = node_shift(picked, -1)
    matrix = assemble(connect, cell_matrix, owned + faces.shape[1], partial)
    returned = node_shift(apply_back(matrix, states, ghosts), 1)

    over_y = jnp.sum(pieces.reshape(4, 2, block // 8, owned), axis=0)
    over_y = jnp.concatenate(
        [jnp.where(first, over_y[0], over_y[1]), jnp.where(first, over_y[1], over_y[0])], axis=1
    )
    over_y, returned, *matrix = tie(over_y, returned, *matrix)
    both = jnp.sum(swap(over_y.reshape(4, block // 32, 2 * owned), "zh"), axis=0)

    mine = apply_cells(matrix, states, ghosts, returned, faces, node_mass)
    other = [ring(weight, "core", 1) for weight in mine]

    own, theirs = both[:, :owned], ring(both[:, owned:], "core", 1)
    rotated = jnp.concatenate(
        [jnp.where(first, own, theirs), jnp.where(first, theirs, own)], axis=0
    )

    group = lax.all_gather(both, "zh", axis=0, tiled=True)
    rows = swap(jnp.broadcast_to(group[None], (4,) + group.shape), "y")
    rows = rows.reshape(block // 2, 2 * owned)
    panel = jnp.concatenate(
        [
            sum(
                jnp.dot(part, weight, precision=HIGH, preferred_element_type=F32)
                for part, weight in ((rows[:, :owned], here), (rows[:, owned:], there))
            )
            for here, there in zip(mine, other)
        ],
        axis=1,
    )
    panel = jnp.sum(swap(panel.reshape(4, block // 8, 2 * width), "x"), axis=0)
    panel = swap(panel.reshape(4, block // 32, 2 * width), "zl")
    return rotated, jnp.sum(panel[:, :, :width], axis=0), jnp.sum(panel[:, :, width:], axis=0)


def solution(mesh):
    fine = Mesh(mesh.devices.reshape(4, 4, 2, 4, 4), FINE)
    return jax.shard_map(
        local,
        mesh=fine,
        in_specs=(
            P(NODE, STATE),
            P(STATE, None),
            P(NODE, None, None),
            P(NODE, None),
            P(NODE),
            P(NODE),
        ),
        out_specs=(P(STATE, NODE), P(NODE, STATE), P(NODE, STATE)),
        check_vma=False,
    )
```
